32 devices in a mesh: grp: 2 (over y), row: 4 (over z), col: 2 (over x), rep: 2 (over core).
Axes of the slice: x: 2, y: 2, z: 4, core: 2. Of those that a mesh axis runs over, the one named last changes fastest.
Arguments:
- emb_row: bfloat16 [2048, 1280], P(('grp', 'row', 'rep'), 'col'), parts along dimension 0, may hold values from -6 to 6
- emb_col: bfloat16 [512, 1280], P(('grp', 'col'), 'row'), parts along dimension 0, may hold values from -6 to 6
- proj_row: bfloat16 [1280, 64], replicated, may hold values from -0.15625 to 0.15625
- proj_col: bfloat16 [1280, 64], replicated, may hold values from -0.15625 to 0.15625
- pair_out: bfloat16 [64, 64], replicated, may hold values from -0.75 to 0.75
- pair_bias: float32 [64], replicated, may hold values from -3 to 3
- conv_weight: bfloat16 [3, 3, 64, 64], replicated, may hold values from -0.25 to 0.25
- conv_bias: float32 [64], replicated, may hold values from -3 to 3
- target: bfloat16 [64, 2048, 256], P(None, ('grp', 'row', 'rep'), 'col'), parts along dimension 1, may hold values from -6 to 6
- kept_tiles: int32 [16, 2], P(('grp', 'row', 'rep'), 'col'), parts along dimension 0, may hold values 0 or 1
Outputs:
- cell_loss: float32 [2048, 256], P(('grp', 'row', 'rep'), 'col'), parts along dimension 0
- grad_conv: float32 [6, 3, 64, 64], P('grp'), parts along dimension 0
- grad_bias: float32 [128], P('grp'), parts along dimension 0
The draws below stay inside these ranges and needn't reach their ends.
There are 2 independent parts, one for each index of `grp`. The reference program is written for one: setup_inputs(seed, part) draws one part's arguments, and reference() takes and returns one part's arrays. A program takes and returns all parts, laid end to end along the dimension named above; an argument that names none is the same for every part. Nothing has to cross between parts.
All inputs are finite; a program needn't handle non-finite values. No bound on the sum of `kept_tiles` on one device may be relied on, other than what follows from the above.
Results may differ from the reference program's by a relative error of at most 0.0025.
Values may be sent and summed in bfloat16 or wider, within the bound.
No kernel may reach another device: no remote copies, remote signals or barrier semaphores. Data moves between devices by JAX's collectives and lax.ppermute only.
A program may use at most 128 MiB of HBM per device.

```python
import jax
import jax.numpy as jnp
from jax import lax

EMBED = 1280
RANK = 64
CHANNELS = 64
TILE_EDGE = 128
ROWS_ALL = 1024
COLS_ALL = 256
TILE_ROWS = 8
TILE_COLS = 2


def touch_ends(result, rng, least, high):
    index_at = [jax.random.randint(jax.random.fold_in(rng, axis), (), 0, length) for axis, length in enumerate(result.shape)]
    widest = result.shape.index(max(result.shape))
    next_to = index_at[:widest] + [(index_at[widest] + 1) % result.shape[widest]] + index_at[widest + 1:]
    return result.at[tuple(index_at)].set(least).at[tuple(next_to)].set(high)


def block_scale(own_key, shape, pieces, least, largest):
    def one(dim, shards_of):
        draws = jax.random.uniform(jax.random.fold_in(jax.random.fold_in(own_key, 6), dim), (shards_of,), jnp.float32, least / len(pieces), largest / len(pieces))
        return jnp.repeat(jnp.exp(draws), shape[dim] // shards_of).reshape((-1,) + (1,) * (len(shape) - dim - 1))

    gain = one(*pieces[0])
    for cut in pieces[1:]:
        gain = gain * one(*cut)
    return gain


def centred(key, extent, scale, bound, cuts=(), held_as=jnp.bfloat16):
    values = jax.random.normal(key, extent, jnp.float32) * scale
    if len(cuts) > 0:
        values = block_scale(key, extent, cuts, -0.22, 0.18) * values
    return jnp.clip(values, min=-bound, max=bound).astype(held_as)


def setup_inputs(seed: int = 0, part: int = 0) -> dict:
    key_list = jax.random.split(jax.random.key(seed), 11)
    own_keys = jax.random.split(jax.random.fold_in(key_list[10], part), 11)
    return {
        "emb_row": centred(own_keys[0], (ROWS_ALL, EMBED), 1.0, 6.0, ((0, 8), (1, 2))),
        "emb_col": centred(own_keys[1], (COLS_ALL, EMBED), 1.0, 6.0, ((0, 2), (1, 4))),
        "proj_row": centred(key_list[2], (EMBED, RANK), EMBED ** -0.5, 0.15625),
        "proj_col": centred(key_list[3], (EMBED, RANK), EMBED ** -0.5, 0.15625),
        "pair_out": centred(key_list[4], (RANK, CHANNELS), RANK ** -0.5, 0.75),
        "pair_bias": centred(key_list[5], (CHANNELS,), 0.5, 3.0, (), jnp.float32),
        "conv_weight": centred(key_list[6], (3, 3, CHANNELS, CHANNELS), (9 * CHANNELS) ** -0.5, 0.25),
        "conv_bias": centred(key_list[7], (CHANNELS,), 0.5, 3.0, (), jnp.float32),
        "target": centred(own_keys[8], (CHANNELS, ROWS_ALL, COLS_ALL), 1.0, 6.0, ((1, 8), (2, 2))),
        "kept_tiles": touch_ends((jax.random.randint(own_keys[9], (TILE_ROWS, TILE_COLS), 0, 4) < 3).astype(jnp.int32), jax.random.fold_in(own_keys[9], 1), 0, 1),
    }


def expand_tiles(tiles, edge):
    count_r, count_c = tiles.shape
    wide = jnp.broadcast_to(tiles.astype(jnp.float32)[:, None, :, None], (count_r, edge, count_c, edge))
    return wide.reshape(count_r * edge, count_c * edge)


def block_terms(padded, pair_feat, target_part, mask, conv_weight, conv_bias):
    rows = pair_feat.shape[1]
    width = pair_feat.shape[2]
    conv_out = jnp.broadcast_to(conv_bias[:, None, None], pair_feat.shape)
    for row_tap in range(3):
        for col_tap in range(3):
            window = padded[:, 2 * row_tap:2 * row_tap + rows, 2 * col_tap:2 * col_tap + width].astype(jnp.float32)
            conv_out = conv_out + jnp.einsum("co,cij->oij", conv_weight[row_tap, col_tap].astype(jnp.float32), window)
    differ = mask[None] * (pair_feat + conv_out - target_part.astype(jnp.float32))
    loss_part = 0.5 * jnp.sum(differ * differ, axis=0)
    grad_in = differ.astype(jnp.bfloat16).astype(jnp.float32)
    taps = []
    for row_tap in range(3):
        for col_tap in range(3):
            window = padded[:, 2 * row_tap:2 * row_tap + rows, 2 * col_tap:2 * col_tap + width].astype(jnp.float32)
            taps.append(jnp.einsum("cij,oij->co", window, grad_in))
    grads = jnp.stack(taps).reshape(3, 3, pair_feat.shape[0], pair_feat.shape[0])
    return loss_part, grads, jnp.sum(differ, axis=(1, 2))


def reference(emb_row, emb_col, proj_row, proj_col, pair_out, pair_bias, conv_weight, conv_bias, target, kept_tiles):
    row_feat = jnp.dot(emb_row, proj_row, preferred_element_type=jnp.float32).astype(jnp.bfloat16)
    col_feat = jnp.dot(emb_col, proj_col, preferred_element_type=jnp.float32).astype(jnp.bfloat16)
    mask = expand_tiles(kept_tiles, TILE_EDGE)
    row_pad = jnp.pad(row_feat, ((2, 2), (0, 0)))
    mask_pad = jnp.pad(mask, ((2, 2), (0, 0)))
    col_wide = col_feat.astype(jnp.float32)
    out_wide = pair_out.astype(jnp.float32)

    def one_block(index):
        start = (index * TILE_EDGE).astype(jnp.int32)
        feats = lax.dynamic_slice_in_dim(row_pad, start, TILE_EDGE + 4, 0)
        mask_rows = lax.dynamic_slice_in_dim(mask_pad, start, TILE_EDGE + 4, 0)
        scaled = (out_wide.T[:, :, None] * feats.astype(jnp.float32).T[None, :, :]).astype(jnp.bfloat16)
        feat_ext = jnp.einsum("cki,jk->cij", scaled.astype(jnp.float32), col_wide) + pair_bias[:, None, None]
        hidden = (jnp.maximum(feat_ext, 0.0) * mask_rows[None]).astype(jnp.bfloat16)
        padded = jnp.pad(hidden, ((0, 0), (0, 0), (2, 2)))
        pair_feat = feat_ext[:, 2:TILE_EDGE + 2]
        mask_here = mask_rows[2:TILE_EDGE + 2]
        target_part = lax.dynamic_slice_in_dim(target, start, TILE_EDGE, 1)
        return block_terms(padded, pair_feat, target_part, mask_here, conv_weight, conv_bias)

    losses, grads, biases = lax.map(one_block, jnp.arange(ROWS_ALL // TILE_EDGE).astype(jnp.int32))
    norm = 1.0 / (TILE_EDGE * TILE_EDGE)
    cell_loss = losses.reshape(ROWS_ALL, COLS_ALL)
    return cell_loss, jnp.sum(grads, axis=0) * norm, jnp.sum(biases, axis=0) * norm
```

```python
import functools

import jax
import jax.numpy as jnp
from jax import lax
from jax.experimental import pallas as pl
from jax.experimental.pallas import tpu as pltpu
from jax.sharding import PartitionSpec as P

REACH = 2
F32 = jnp.float32
BF16 = jnp.bfloat16


def swap(x, axis, step):
    size = lax.axis_size(axis)
    return lax.ppermute(x, axis, [(i, i ^ step) for i in range(size)])


def steps(axis):
    size, step = lax.axis_size(axis), 1
    while step < size:
        yield step
        step *= 2


def tile_kernel(
    row_ref, rhs_ref, mask_ref, out_ref, pbias_ref, weight_ref, cbias_ref, target_ref,
    loss_ref, grad_ref, hid, dif_taps, feat, near, far, bias_sum, acc, *, norm
):
    chans, width = feat.shape[1], feat.shape[2]
    cols = width // 2
    pairs = feat.shape[0]
    taps = weight_ref.shape[0]
    lane = lax.broadcasted_iota(jnp.int32, (chans, cols), 1)
    pair_out = out_ref[...]
    pbias = jnp.broadcast_to(pbias_ref[...], (chans, width))
    pbias = jnp.concatenate([pbias, pbias], axis=0)

    def features(e, carry):
        zone = jnp.where(e == 0, 0, jnp.where(e == pairs - 1, 2, 1))
        mask = mask_ref[pl.ds(zone, 1), :]
        two = row_ref[e]
        scaled = jnp.concatenate([pair_out * two[0:1], pair_out * two[1:2]], axis=0).astype(BF16)
        value = jnp.dot(scaled, rhs_ref[...], preferred_element_type=F32) + pbias
        hidden = jnp.maximum(value, 0.0) * mask
        for h in range(2):
            part = slice(h * chans, (h + 1) * chans)
            place = pl.ds(pl.multiple_of(e * width + h * cols, 128), cols)
            feat[e, :, h * cols:(h + 1) * cols] = value[part, :cols]
            own, beside = hidden[part, :cols], hidden[part, cols:]
            before = pltpu.roll(jnp.where(lane >= cols - REACH, beside, own), REACH, 1)
            after = pltpu.roll(jnp.where(lane < REACH, beside, own), cols - REACH, 1)
            hid[0:chans, place] = before.astype(BF16)
            hid[chans:2 * chans, place] = own.astype(BF16)
            hid[2 * chans:3 * chans, place] = after.astype(BF16)
        return carry

    lax.fori_loop(0, pairs, features, 0, unroll=2)

    def conv(e):
        place = pl.ds(pl.multiple_of(e * width, 128), width)
        return jnp.dot(weight_ref[...], hid[:, place], preferred_element_type=F32)

    zero = jnp.zeros((chans, width), BF16)
    for tap, e in ((0, pairs - 2), (0, pairs - 1), (1, 0), (1, pairs - 1), (2, 0), (2, 1)):
        dif_taps[tap * chans:(tap + 1) * chans, e * width:(e + 1) * width] = zero
    cbias = jnp.broadcast_to(cbias_ref[...], (chans, width))
    keep = mask_ref[3:4, :]
    bias_sum[...] = jnp.zeros_like(bias_sum)
    first, second = conv(0), conv(1)
    near[...] = first[0:chans] + second[chans:2 * chans]
    far[...] = second[0:chans]

    def differences(e, carry):
        m = e - 2
        part = conv(e)
        out = near[...] + part[2 * chans:]
        near[...] = far[...] + part[chans:2 * chans]
        far[...] = part[0:chans]
        target = jnp.concatenate([target_ref[2 * m], target_ref[2 * m + 1]], axis=1).astype(F32)
        differ = keep * (feat[e - 1] + (out + cbias) - target)
        loss = 0.5 * jnp.sum(differ * differ, axis=0, keepdims=True)
        loss_ref[pl.ds(2 * m, 1), :] = loss[:, :cols]
        loss_ref[pl.ds(2 * m + 1, 1), :] = loss[:, cols:]
        bias_sum[...] += differ
        rounded = differ.astype(BF16)
        for tap in range(3):
            place = pl.ds(pl.multiple_of((m + tap) * width, 128), width)
            dif_taps[tap * chans:(tap + 1) * chans, place] = rounded
        return carry

    lax.fori_loop(2, pairs, differences, 0, unroll=2)

    chunk = width * 6 if pairs % 6 == 0 else width
    acc[...] = jnp.zeros_like(acc)

    def gradients(s, carry):
        place = pl.ds(pl.multiple_of(s * chunk, 128), chunk)
        acc[...] += lax.dot_general(
            hid[:, place], dif_taps[:, place], (((1,), (1,)), ((), ())), preferred_element_type=F32
        )
        return carry

    lax.fori_loop(0, pairs * width // chunk, gradients, 0)
    half = taps // 2
    grad_ref[0:taps, :] = acc[:, 0:2 * chans] * norm
    last = acc[:, 2 * chans:] * norm
    grad_ref[taps:taps + half, :] = jnp.concatenate([last[:half], last[half:]], axis=1)
    sums = bias_sum[:, :cols] + bias_sum[:, cols:]
    ones = jnp.ones((8, cols), F32)
    bias = lax.dot_general(
        ones, sums, (((1,), (1,)), ((), ())), preferred_element_type=F32, precision=lax.Precision.HIGHEST
    )
    grad_ref[taps + half:, :] = jnp.zeros((grad_ref.shape[0] - taps - half, 2 * chans), F32)
    grad_ref[taps + half:taps + half + 8, 0:chans] = bias * norm


def per_device(
    emb_row, emb_col, proj_row, proj_col, pair_out, pair_bias, conv_weight, conv_bias, target, kept_tiles
):
    chans, rows, cols = target.shape
    rank = pair_out.shape[0]
    row, col, rep = lax.axis_index("row"), lax.axis_index("col"), lax.axis_index("rep")
    n_row, n_col, n_rep = lax.axis_size("row"), lax.axis_size("col"), lax.axis_size("rep")
    edge = rows // kept_tiles.shape[0]
    half = rows // 2

    share = emb_row.shape[1]
    row_part = jnp.dot(
        emb_row, lax.dynamic_slice_in_dim(proj_row, col * share, share, 0), preferred_element_type=F32
    )
    share = emb_col.shape[1]
    col_part = lax.dot_general(
        lax.dynamic_slice_in_dim(proj_col, row * share, share, 0), emb_col,
        (((0,), (1,)), ((), ())), preferred_element_type=F32,
    )
    row_part = jnp.concatenate([row_part[:half], row_part[half:]], axis=1)
    kept = jnp.broadcast_to(kept_tiles.astype(F32), (8, cols))

    send = jnp.concatenate([row_part, col_part, kept], axis=0)
    row_sum = row_part
    near_by = {}
    for k in range(1, n_col):
        got = lax.ppermute(send, "col", [(i, (i + k) % n_col) for i in range(n_col)])
        row_sum = row_sum + got[:half]
        near_by[k] = got[half:]
    left, right = near_by[1], near_by[n_col - 1]
    lane = lax.broadcasted_iota(jnp.int32, (rank, cols), 1)
    side = jnp.where(lane >= cols - REACH, left[:rank], jnp.where(lane < REACH, right[:rank], 0.0))
    lane = lax.broadcasted_iota(jnp.int32, (1, cols), 1)
    side_mask = jnp.where(
        (lane >= cols - REACH) & (col > 0), left[rank:rank + 1],
        jnp.where((lane < REACH) & (col < n_col - 1), right[rank:rank + 1], 0.0),
    )

    own = jnp.concatenate(
        [row_sum[:REACH], row_sum[half - REACH:], kept[:1], side_mask, jnp.zeros((2, cols), F32)], axis=0
    )
    other = swap(own, "rep", 1)
    edges = jnp.concatenate([jnp.where(rep == 0, own, other), jnp.where(rep == 0, other, own)], axis=0)
    col_sum = jnp.concatenate([col_part, side], axis=0)
    for step in steps("row"):
        got = swap(jnp.concatenate([col_sum, edges], axis=0), "row", step)
        col_sum = col_sum + got[:2 * rank]
        edges = jnp.concatenate([edges, got[2 * rank:]], axis=0)

    block = row * n_rep + rep

    def beside(index):
        inside = (index >= 0) & (index < n_row * n_rep)
        index = jnp.clip(index, 0, n_row * n_rep - 1)
        place = ((index // n_rep) ^ row) * n_rep + index % n_rep
        found = lax.dynamic_slice_in_dim(edges, place * 8, 8, 0)
        mask = jnp.concatenate([found[4:5], found[5:6]], axis=1)
        return found, jnp.where(inside, mask, 0.0)

    above, above_mask = beside(block - 1)
    below, below_mask = beside(block + 1)
    row_feat = jnp.concatenate(
        [above[REACH:2 * REACH, rank:], row_sum[:, :rank], row_sum[:, rank:], below[:REACH, :rank]], axis=0
    ).astype(BF16).astype(F32).reshape(half + REACH, 2, rank)
    rhs = jnp.concatenate([col_sum[:rank], col_sum[rank:]], axis=1).astype(BF16)
    own_mask = jnp.concatenate([kept[:1], side_mask], axis=1)
    all_kept = jnp.concatenate([kept[:1], kept[:1]], axis=1)
    masks = jnp.concatenate(
        [above_mask, own_mask, below_mask, all_kept, jnp.zeros((4, 2 * cols), F32)], axis=0
    )

    pairs = half + REACH
    width = 2 * cols
    taps = 3 * chans
    weight = conv_weight.transpose(0, 3, 1, 2).reshape(taps, taps)
    packed = taps + taps // 2 + 16
    cell_loss, grads = pl.pallas_call(
        functools.partial(tile_kernel, norm=1.0 / (edge * edge)),
        out_shape=(
            jax.ShapeDtypeStruct((rows, cols), F32),
            jax.ShapeDtypeStruct((packed, 2 * chans), F32),
        ),
        in_specs=[pl.BlockSpec(memory_space=pltpu.VMEM)] * 8,
        out_specs=(pl.BlockSpec(memory_space=pltpu.VMEM),) * 2,
        scratch_shapes=[
            pltpu.VMEM((taps, pairs * width), BF16),
            pltpu.VMEM((taps, pairs * width), BF16),
            pltpu.VMEM((pairs, chans, width), F32),
            pltpu.VMEM((chans, width), F32),
            pltpu.VMEM((chans, width), F32),
            pltpu.VMEM((chans, width), F32),
            pltpu.VMEM((taps, taps), F32),
        ],
        compiler_params=pltpu.CompilerParams(vmem_limit_bytes=40 * 1024 * 1024),
        name="tile",
    )(
        row_feat, rhs, masks, pair_out.astype(F32).T, pair_bias[:, None], weight,
        conv_bias[:, None], target.transpose(1, 0, 2),
    )

    piece = packed // n_rep
    mine = lax.dynamic_slice_in_dim(grads, rep * piece, piece, 0)
    total = mine + swap(lax.dynamic_slice_in_dim(grads, (1 - rep) * piece, piece, 0), "rep", 1)
    for axis in ("col", "row"):
        for step in steps(axis):
            total = total + swap(total, axis, step)
    other = swap(total, "rep", 1)
    grads = jnp.concatenate([jnp.where(rep == 0, total, other), jnp.where(rep == 0, other, total)], axis=0)
    main = grads[:taps].reshape(3, chans, 2, chans).transpose(2, 0, 1, 3)
    last = grads[taps:taps + taps // 2]
    last = jnp.concatenate([last[:, :chans], last[:, chans:]], axis=0).reshape(1, 3, chans, chans)
    grad_conv = jnp.concatenate([main, last], axis=0)
    grad_bias = grads[taps + taps // 2, :chans]
    return cell_loss, grad_conv, grad_bias


def solution(mesh):
    in_specs = (
        P(("grp", "row", "rep"), "col"),
        P(("grp", "col"), "row"),
        P(),
        P(),
        P(),
        P(),
        P(),
        P(),
        P(None, ("grp", "row", "rep"), "col"),
        P(("grp", "row", "rep"), "col"),
    )
    out_specs = (P(("grp", "row", "rep"), "col"), P("grp", None, None, None), P("grp"))
    return jax.shard_map(
        per_device, mesh=mesh, in_specs=in_specs, out_specs=out_specs, check_vma=False
    )
```

```python
import functools

import jax
import jax.numpy as jnp
from jax import lax
from jax.experimental import pallas as pl
from jax.experimental.pallas import tpu as pltpu
from jax.sharding import PartitionSpec as P

REACH = 2
F32 = jnp.float32
BF16 = jnp.bfloat16


def swap(x, axis, step):
    size = lax.axis_size(axis)
    return lax.ppermute(x, axis, [(i, i ^ step) for i in range(size)])


def steps(axis):
    size, step = lax.axis_size(axis), 1
    while step < size:
        yield step
        step *= 2


def tile_kernel(
    row_ref, rhs_ref, mask_ref, out_ref, pbias_ref, weight_ref, cbias_ref, target_ref,
    loss_ref, grad_ref, hid, dif_taps, feat, near, far, bias_sum, *, norm
):
    chans, width = feat.shape[1], feat.shape[2]
    cols = width // 2
    pairs = feat.shape[0]
    taps = weight_ref.shape[0]
    lane = lax.broadcasted_iota(jnp.int32, (chans, cols), 1)
    pair_out = out_ref[...]
    pbias = jnp.broadcast_to(pbias_ref[...], (chans, width))
    pbias = jnp.concatenate([pbias, pbias], axis=0)

    def features(e, carry):
        zone = jnp.where(e == 0, 0, jnp.where(e == pairs - 1, 2, 1))
        mask = mask_ref[pl.ds(zone, 1), :]
        two = row_ref[e]
        scaled = jnp.concatenate([pair_out * two[0:1], pair_out * two[1:2]], axis=0).astype(BF16)
        value = jnp.dot(scaled, rhs_ref[...], preferred_element_type=F32) + pbias
        hidden = jnp.maximum(value, 0.0) * mask
        for h in range(2):
            part = slice(h * chans, (h + 1) * chans)
            place = pl.ds(pl.multiple_of(e * width + h * cols, 128), cols)
            feat[e, :, h * cols:(h + 1) * cols] = value[part, :cols]
            own, beside = hidden[part, :cols], hidden[part, cols:]
            before = pltpu.roll(jnp.where(lane >= cols - REACH, beside, own), REACH, 1)
            after = pltpu.roll(jnp.where(lane < REACH, beside, own), cols - REACH, 1)
            hid[0:chans, place] = before.astype(BF16)
            hid[chans:2 * chans, place] = own.astype(BF16)
            hid[2 * chans:3 * chans, place] = after.astype(BF16)
        return carry

    lax.fori_loop(0, pairs, features, 0, unroll=pairs)

    def conv(e):
        place = pl.ds(pl.multiple_of(e * width, 128), width)
        return jnp.dot(weight_ref[...], hid[:, place], preferred_element_type=F32)

    zero = jnp.zeros((chans, width), BF16)
    for tap, e in ((0, pairs - 2), (0, pairs - 1), (1, 0), (1, pairs - 1), (2, 0), (2, 1)):
        dif_taps[tap * chans:(tap + 1) * chans, e * width:(e + 1) * width] = zero
    cbias = jnp.broadcast_to(cbias_ref[...], (chans, width))
    keep = mask_ref[3:4, :]
    bias_sum[...] = jnp.zeros_like(bias_sum)
    first, second = conv(0), conv(1)
    near[...] = first[0:chans] + second[chans:2 * chans]
    far[...] = second[0:chans]

    def differences(e, carry):
        m = e - 2
        part = conv(e)
        out = near[...] + part[2 * chans:]
        near[...] = far[...] + part[chans:2 * chans]
        far[...] = part[0:chans]
        target = jnp.concatenate([target_ref[2 * m], target_ref[2 * m + 1]], axis=1).astype(F32)
        differ = keep * (feat[e - 1] + (out + cbias) - target)
        loss = 0.5 * jnp.sum(differ * differ, axis=0, keepdims=True)
        loss_ref[pl.ds(2 * m, 1), :] = loss[:, :cols]
        loss_ref[pl.ds(2 * m + 1, 1), :] = loss[:, cols:]
        bias_sum[...] += differ
        rounded = differ.astype(BF16)
        for tap in range(3):
            place = pl.ds(pl.multiple_of((m + tap) * width, 128), width)
            dif_taps[tap * chans:(tap + 1) * chans, place] = rounded
        return carry

    lax.fori_loop(2, pairs, differences, 0, unroll=pairs - 2)

    grad = lax.dot_general(
        hid[...], dif_taps[...], (((1,), (1,)), ((), ())), preferred_element_type=F32
    ) * norm
    half = taps // 2
    grad_ref[0:taps, :] = grad[:, 0:2 * chans]
    last = grad[:, 2 * chans:]
    grad_ref[taps:taps + half, :] = jnp.concatenate([last[:half], last[half:]], axis=1)
    sums = bias_sum[:, :cols] + bias_sum[:, cols:]
    ones = jnp.ones((8, cols), F32)
    bias = lax.dot_general(
        ones, sums, (((1,), (1,)), ((), ())), preferred_element_type=F32, precision=lax.Precision.HIGHEST
    )
    grad_ref[taps + half:, :] = jnp.zeros((grad_ref.shape[0] - taps - half, 2 * chans), F32)
    grad_ref[taps + half:taps + half + 8, 0:chans] = bias * norm


def per_device(
    emb_row, emb_col, proj_row, proj_col, pair_out, pair_bias, conv_weight, conv_bias, target, kept_tiles
):
    chans, rows, cols = target.shape
    rank = pair_out.shape[0]
    row, col, rep = lax.axis_index("row"), lax.axis_index("col"), lax.axis_index("rep")
    n_row, n_col, n_rep = lax.axis_size("row"), lax.axis_size("col"), lax.axis_size("rep")
    edge = rows // kept_tiles.shape[0]
    half = rows // 2

    share = emb_row.shape[1]
    row_part = jnp.dot(
        emb_row, lax.dynamic_slice_in_dim(proj_row, col * share, share, 0), preferred_element_type=F32
    )
    share = emb_col.shape[1]
    col_part = lax.dot_general(
        lax.dynamic_slice_in_dim(proj_col, row * share, share, 0), emb_col,
        (((0,), (1,)), ((), ())), preferred_element_type=F32,
    )
    row_part = jnp.concatenate([row_part[:half], row_part[half:]], axis=1)
    kept = jnp.broadcast_to(kept_tiles.astype(F32), (8, cols))

    send = jnp.concatenate([row_part, col_part, kept], axis=0)
    row_sum = row_part
    near_by = {}
    for k in range(1, n_col):
        got = lax.ppermute(send, "col", [(i, (i + k) % n_col) for i in range(n_col)])
        row_sum = row_sum + got[:half]
        near_by[k] = got[half:]
    left, right = near_by[1], near_by[n_col - 1]
    lane = lax.broadcasted_iota(jnp.int32, (rank, cols), 1)
    side = jnp.where(lane >= cols - REACH, left[:rank], jnp.where(lane < REACH, right[:rank], 0.0))
    lane = lax.broadcasted_iota(jnp.int32, (1, cols), 1)
    side_mask = jnp.where(
        (lane >= cols - REACH) & (col > 0), left[rank:rank + 1],
        jnp.where((lane < REACH) & (col < n_col - 1), right[rank:rank + 1], 0.0),
    )

    own = jnp.concatenate(
        [row_sum[:REACH], row_sum[half - REACH:], kept[:1], side_mask, jnp.zeros((2, cols), F32)], axis=0
    )
    other = swap(own, "rep", 1)
    edges = jnp.concatenate([jnp.where(rep == 0, own, other), jnp.where(rep == 0, other, own)], axis=0)
    col_sum = jnp.concatenate([col_part, side], axis=0)
    for step in steps("row"):
        got = swap(jnp.concatenate([col_sum, edges], axis=0), "row", step)
        col_sum = col_sum + got[:2 * rank]
        edges = jnp.concatenate([edges, got[2 * rank:]], axis=0)

    block = row * n_rep + rep

    def beside(index):
        inside = (index >= 0) & (index < n_row * n_rep)
        index = jnp.clip(index, 0, n_row * n_rep - 1)
        place = ((index // n_rep) ^ row) * n_rep + index % n_rep
        found = lax.dynamic_slice_in_dim(edges, place * 8, 8, 0)
        mask = jnp.concatenate([found[4:5], found[5:6]], axis=1)
        return found, jnp.where(inside, mask, 0.0)

    above, above_mask = beside(block - 1)
    below, below_mask = beside(block + 1)
    row_feat = jnp.concatenate(
        [above[REACH:2 * REACH, rank:], row_sum[:, :rank], row_sum[:, rank:], below[:REACH, :rank]], axis=0
    ).astype(BF16).astype(F32).reshape(half + REACH, 2, rank)
    rhs = jnp.concatenate([col_sum[:rank], col_sum[rank:]], axis=1).astype(BF16)
    own_mask = jnp.concatenate([kept[:1], side_mask], axis=1)
    all_kept = jnp.concatenate([kept[:1], kept[:1]], axis=1)
    masks = jnp.concatenate(
        [above_mask, own_mask, below_mask, all_kept, jnp.zeros((4, 2 * cols), F32)], axis=0
    )

    pairs = half + REACH
    width = 2 * cols
    taps = 3 * chans
    weight = conv_weight.transpose(0, 3, 1, 2).reshape(taps, taps)
    packed = taps + taps // 2 + 16
    cell_loss, grads = pl.pallas_call(
        functools.partial(tile_kernel, norm=1.0 / (edge * edge)),
        out_shape=(
            jax.ShapeDtypeStruct((rows, cols), F32),
            jax.ShapeDtypeStruct((packed, 2 * chans), F32),
        ),
        in_specs=[pl.BlockSpec(memory_space=pltpu.VMEM)] * 8,
        out_specs=(pl.BlockSpec(memory_space=pltpu.VMEM),) * 2,
        scratch_shapes=[
            pltpu.VMEM((taps, pairs * width), BF16),
            pltpu.VMEM((taps, pairs * width), BF16),
            pltpu.VMEM((pairs, chans, width), F32),
            pltpu.VMEM((chans, width), F32),
            pltpu.VMEM((chans, width), F32),
            pltpu.VMEM((chans, width), F32),
        ],
        compiler_params=pltpu.CompilerParams(vmem_limit_bytes=40 * 1024 * 1024),
        name="tile",
    )(
        row_feat, rhs, masks, pair_out.astype(F32).T, pair_bias[:, None], weight,
        conv_bias[:, None], target.transpose(1, 0, 2),
    )

    piece = packed // n_rep
    mine = lax.dynamic_slice_in_dim(grads, rep * piece, piece, 0)
    total = mine + swap(lax.dynamic_slice_in_dim(grads, (1 - rep) * piece, piece, 0), "rep", 1)
    for axis in ("col", "row"):
        for step in steps(axis):
            total = total + swap(total, axis, step)
    other = swap(total, "rep", 1)
    grads = jnp.concatenate([jnp.where(rep == 0, total, other), jnp.where(rep == 0, other, total)], axis=0)
    main = grads[:taps].reshape(3, chans, 2, chans).transpose(2, 0, 1, 3)
    last = grads[taps:taps + taps // 2]
    last = jnp.concatenate([last[:, :chans], last[:, chans:]], axis=0).reshape(1, 3, chans, chans)
    grad_conv = jnp.concatenate([main, last], axis=0)
    grad_bias = grads[taps + taps // 2, :chans]
    return cell_loss, grad_conv, grad_bias


def solution(mesh):
    in_specs = (
        P(("grp", "row", "rep"), "col"),
        P(("grp", "col"), "row"),
        P(),
        P(),
        P(),
        P(),
        P(),
        P(),
        P(None, ("grp", "row", "rep"), "col"),
        P(("grp", "row", "rep"), "col"),
    )
    out_specs = (P(("grp", "row", "rep"), "col"), P("grp", None, None, None), P("grp"))
    return jax.shard_map(
        per_device, mesh=mesh, in_specs=in_specs, out_specs=out_specs, check_vma=False
    )
```

```python
import functools

import jax
import jax.numpy as jnp
from jax import lax
from jax.experimental import pallas as pl
from jax.experimental.pallas import tpu as pltpu
from jax.sharding import PartitionSpec as P

REACH = 2
F32 = jnp.float32
BF16 = jnp.bfloat16
ROWS_BY_COLS = (((1,), (1,)), ((), ()))
MESH = ("row", "col", "rep")


def swap(x, row=0, col=0, rep=0):
    sizes = [lax.axis_size(axis) for axis in MESH]

    def index(r, c, p):
        return (r * sizes[1] + c) * sizes[2] + p

    places = [(r, c, p) for r in range(sizes[0]) for c in range(sizes[1]) for p in range(sizes[2])]
    return lax.ppermute(
        x, MESH, [(index(r, c, p), index(r ^ row, c ^ col, p ^ rep)) for r, c, p in places]
    )


def steps(axis, first=1):
    step = first
    while step < lax.axis_size(axis):
        yield step
        step *= 2


def zeros_kernel(zeros_ref):
    zeros_ref[...] = jnp.zeros_like(zeros_ref)


def project_kernel(
    zeros_ref, kept_ref, row_ref, row_proj_ref, col_ref, col_proj_ref,
    col_send_ref, row_send_ref, cross_send_ref, col_wide, *, sliced
):
    row_at = col_at = 0
    depth = row_ref.shape[1]
    if sliced[0]:
        row_at = pl.multiple_of(lax.axis_index("col") * depth, 128)
    if sliced[1]:
        col_at = pl.multiple_of(lax.axis_index("row") * col_ref.shape[0], 16)
    col_wide[...] = jnp.zeros_like(col_wide)
    col_wide[pl.ds(col_at, col_ref.shape[0]), :] = col_ref[...]
    half, wide = row_ref.shape[0] // 2, 2 * row_proj_ref.shape[0]
    lane = lax.broadcasted_iota(jnp.int32, (REACH, wide), 1)

    def packed(x):
        return jnp.concatenate([x[:half], x[half:]], axis=1)

    def ends(x):
        return jnp.where(lane < wide // 2, x[:REACH], x[half - REACH:])

    kept = jnp.broadcast_to(kept_ref[...].astype(F32), (1, wide))
    rows = packed(
        lax.dot_general(
            row_ref[...], row_proj_ref[:, pl.ds(row_at, depth)], ROWS_BY_COLS, preferred_element_type=F32
        )
    )
    cols = packed(jnp.dot(col_proj_ref[...], col_wide[...], preferred_element_type=F32).T)
    row_ends, col_ends = ends(rows), ends(cols)
    zero = zeros_ref[...]
    col_send_ref[0:half, :] = rows
    row_send_ref[0:half, :] = cols
    col_send_ref[half:, :] = jnp.concatenate([col_ends, kept, zero[:5]], axis=0)
    row_send_ref[half:, :] = jnp.concatenate([row_ends, kept, zero[:5]], axis=0)
    cross_send_ref[...] = jnp.concatenate([row_ends, kept, col_ends, zero[:3]], axis=0)


def tile_kernel(
    row_ref, col_ref, misc_ref, out_ref, pbias_ref, weight_ref, cbias_ref, target_hbm,
    loss_ref, grad_ref, target_ref, sem, hid, dif_taps, feat, rhs, near, far, bias_sum, *, norm
):
    chans, rows, cols = target_ref.shape
    half, wide = row_ref.shape
    rank = wide // 2
    width = 2 * cols
    pairs = rows // 2 + 2
    taps = weight_ref.shape[0]

    target_copy = pltpu.make_async_copy(target_hbm, target_ref, sem)
    target_copy.start()

    rhs[...] = jnp.zeros_like(rhs)
    lane = lax.broadcasted_iota(jnp.int32, (half, wide), 1)
    for start, value in ((0, col_ref[...]), (cols, misc_ref[0:REACH, :])):
        turned = pltpu.roll(value, rank, 1)
        size = value.shape[0]
        lower = lane[:size] < rank
        gap = half if start == 0 else cols - REACH
        for base, first, last in ((0, value, turned), (2 * cols, turned, value)):
            keep_half = lower if base == 0 else ~lower
            at = base + start
            rhs[at:at + size, :] = jnp.where(keep_half, first, 0.0)
            rhs[at + gap:at + gap + size, :] = jnp.where(keep_half, last, 0.0)
    factors = rhs[...].astype(BF16)

    lane = lax.broadcasted_iota(jnp.int32, (chans, cols), 1)
    pair_out = out_ref[...]
    pbias = jnp.broadcast_to(pbias_ref[...], (chans, cols))

    def features(rounded, places):
        scaled = jnp.concatenate([pair_out * rounded[j:j + 1] for j in range(len(places))], axis=0)
        values = lax.dot_general(scaled.astype(BF16), factors, ROWS_BY_COLS, preferred_element_type=F32)
        for j, place in enumerate(places):
            for side, i in enumerate(place):
                value = values[j * chans:(j + 1) * chans, side * width:(side + 1) * width]
                own, beside = value[:, :cols] + pbias, value[:, cols:] + pbias
                if 0 <= i < rows:
                    feat[i // 2, :, (i % 2) * cols:(i % 2 + 1) * cols] = own
                zone = 6 if i < 0 else 8 if i >= rows else 4
                own = jnp.maximum(own, 0.0) * misc_ref[zone:zone + 1, :]
                beside = jnp.maximum(beside, 0.0) * misc_ref[zone + 1:zone + 2, :]
                before = pltpu.roll(jnp.where(lane >= cols - REACH, beside, own), REACH, 1)
                after = pltpu.roll(jnp.where(lane < REACH, beside, own), cols - REACH, 1)
                at = slice((i + REACH) * cols, (i + REACH + 1) * cols)
                hid[0:chans, at] = before.astype(BF16)
                hid[chans:2 * chans, at] = own.astype(BF16)
                hid[2 * chans:3 * chans, at] = after.astype(BF16)

    def rounded(x):
        return x.astype(BF16).astype(F32)

    features(rounded(misc_ref[REACH:2 * REACH, :]), [(rows + j, j - REACH) for j in range(REACH)])
    for m in range(0, half, GROUP):
        features(rounded(row_ref[m:m + GROUP, :]), [(m + j, half + m + j) for j in range(GROUP)])

    target_copy.wait()

    zero = jnp.zeros((chans, width), BF16)
    for tap, e in ((0, pairs - 2), (0, pairs - 1), (1, 0), (1, pairs - 1), (2, 0), (2, 1)):
        dif_taps[tap * chans:(tap + 1) * chans, e * width:(e + 1) * width] = zero
    cbias = jnp.broadcast_to(cbias_ref[...], (chans, width))
    keep = jnp.concatenate([misc_ref[4:5, :]] * 2, axis=1)
    bias_sum[...] = jnp.zeros_like(bias_sum)
    for e in range(pairs):
        part = jnp.dot(weight_ref[...], hid[:, e * width:(e + 1) * width], preferred_element_type=F32)
        m = e - 2
        if m >= 0:
            if (2 * m) % 16 == 0:
                targets = jnp.swapaxes(target_ref[:, 2 * m:2 * m + 16, :], 0, 1)
            at = (2 * m) % 16
            target = jnp.concatenate([targets[at], targets[at + 1]], axis=1).astype(F32)
            out = near[...] + part[2 * chans:]
            differ = keep * (feat[m] + (out + cbias) - target)
            loss = 0.5 * jnp.sum(differ * differ, axis=0, keepdims=True)
            loss_ref[2 * m:2 * m + 1, :] = loss[:, :cols]
            loss_ref[2 * m + 1:2 * m + 2, :] = loss[:, cols:]
            bias_sum[...] += differ
            grad_in = differ.astype(BF16)
            for tap in range(3):
                dif_taps[tap * chans:(tap + 1) * chans, (m + tap) * width:(m + tap + 1) * width] = grad_in
        if e > 0:
            near[...] = far[...] + part[chans:2 * chans]
        far[...] = part[0:chans]

    grad = lax.dot_general(hid[...], dif_taps[...], ROWS_BY_COLS, preferred_element_type=F32) * norm
    split = taps // 2
    grad_ref[0:taps, :] = grad[:, 0:2 * chans]
    last = grad[:, 2 * chans:]
    grad_ref[taps:taps + split, :] = jnp.concatenate([last[:split], last[split:]], axis=1)
    sums = bias_sum[:, :cols] + bias_sum[:, cols:]
    bias = lax.dot_general(
        jnp.ones((8, cols), F32), sums, ROWS_BY_COLS, preferred_element_type=F32, precision=lax.Precision.HIGHEST
    )
    grad_ref[taps + split:, :] = jnp.zeros((grad_ref.shape[0] - taps - split, 2 * chans), F32)
    grad_ref[taps + split:taps + split + 8, 0:chans] = bias * norm


GROUP = 2


def per_device(
    emb_row, emb_col, proj_row, proj_col, pair_out, pair_bias, conv_weight, conv_bias, target, kept_tiles
):
    chans, rows, cols = target.shape
    rank = pair_out.shape[0]
    row, col, rep = (lax.axis_index(axis) for axis in MESH)
    n_row, n_col, n_rep = (lax.axis_size(axis) for axis in MESH)
    edge = rows // kept_tiles.shape[0]
    half, wide = rows // 2, 2 * rank
    vmem = pl.BlockSpec(memory_space=pltpu.VMEM)

    shares = emb_row.shape[1], emb_col.shape[1]
    sliced = (shares[0] % 128 == 0, shares[1] % 16 == 0)
    projs = [proj_row.T, proj_col.T]
    for side, place in enumerate((col, row)):
        if not sliced[side]:
            projs[side] = lax.dynamic_slice_in_dim(projs[side], place * shares[side], shares[side], 1)
    zeros = pl.pallas_call(
        zeros_kernel,
        out_shape=jax.ShapeDtypeStruct((8, wide), F32),
        out_specs=vmem,
        compiler_params=pltpu.CompilerParams(vmem_limit_bytes=4 * 1024 * 1024),
        cost_estimate=pl.CostEstimate(flops=4 * 10**9, bytes_accessed=1000, transcendentals=0),
        name="zeros",
    )()
    col_send, row_send, cross_send = pl.pallas_call(
        functools.partial(project_kernel, sliced=sliced),
        out_shape=(
            jax.ShapeDtypeStruct((half + 8, wide), F32),
            jax.ShapeDtypeStruct((half + 8, wide), F32),
            jax.ShapeDtypeStruct((8, wide), F32),
        ),
        in_specs=[vmem] * 6,
        out_specs=(vmem,) * 3,
        scratch_shapes=[pltpu.VMEM((projs[1].shape[1], cols), BF16)],
        compiler_params=pltpu.CompilerParams(vmem_limit_bytes=4 * 1024 * 1024),
        cost_estimate=pl.CostEstimate(flops=2 * 10**9, bytes_accessed=1000, transcendentals=0),
        name="project",
    )(zeros, kept_tiles, emb_row, projs[0], emb_col.T, projs[1])

    shift = [[(i, (i + k) % n_col) for i in range(n_col)] for k in range(n_col)]
    row_cols = ("row", "col", "rep")

    def cross(x, k):
        def index(r, c, p):
            return (r * n_col + c) * n_rep + p

        return lax.ppermute(
            x, row_cols,
            [
                (index(r, c, p), index(r ^ 1, (c + k) % n_col, p ^ 1))
                for r in range(n_row) for c in range(n_col) for p in range(n_rep)
            ],
        )

    from_cross = {k: cross(cross_send, k) for k in range(1, n_col)}
    from_col = {k: lax.ppermute(col_send, "col", shift[k]) for k in range(1, n_col)}
    from_row = swap(row_send, row=1, rep=1)

    lane = lax.broadcasted_iota(jnp.int32, (1, wide), 1)
    lower = lane < rank

    def sides(blocks, at, size):
        return jnp.where(lower, blocks[n_col - 1][at:at + size], blocks[1][at:at + size])

    def outside(mask):
        return jnp.where(jnp.where(lower, col < n_col - 1, col > 0), mask, 0.0)

    row_sum = col_send[:half] + sum(from_col[k][:half] for k in from_col)
    col_sum = row_send[:half] + from_row[:half]
    side = sides(from_col, half, REACH) + sides(from_cross, REACH + 1, REACH)
    own_kept = col_send[half + REACH:half + REACH + 1]
    own_masks = jnp.concatenate([own_kept, outside(sides(from_col, half + REACH, 1))], axis=0)
    own_ends = jnp.where(lower, row_sum[:REACH], row_sum[half - REACH:])
    block = jnp.concatenate(
        [
            from_row[half:half + REACH] + sum(from_cross[k][:REACH] for k in from_cross),
            from_row[half + REACH:half + REACH + 1],
            outside(sides(from_cross, REACH, 1)),
        ],
        axis=0,
    )
    mate = swap(jnp.concatenate([own_ends, own_masks, jnp.zeros((4, wide), F32)], axis=0), rep=1)

    blocks = {1: block}
    pad = jnp.zeros((2, wide), F32)
    for step in steps("row", 2):
        got = swap(jnp.concatenate([col_sum, side, blocks[step - 1], pad], axis=0), row=step)
        col_sum = col_sum + got[:half]
        side = side + got[half:half + REACH]
        blocks[2 * step - 1] = got[half + REACH:half + REACH + 4]

    beyond = jnp.where(rep == 0, row - 1, row + 1)
    far = blocks[1]
    for apart, found in blocks.items():
        far = jnp.where((row ^ beyond) == apart, found, far)
    far_masks = jnp.where((beyond >= 0) & (beyond < n_row), far[REACH:], 0.0)
    above = jnp.where(rep == 0, far[:REACH], mate[:REACH])
    below = jnp.where(rep == 0, mate[:REACH], far[:REACH])
    mate_masks = mate[REACH:REACH + 2]
    misc = jnp.concatenate(
        [
            side,
            jnp.where(lower, below, above),
            own_masks,
            jnp.where(rep == 0, far_masks, mate_masks),
            jnp.where(rep == 0, mate_masks, far_masks),
            jnp.zeros((6, wide), F32),
        ],
        axis=0,
    )

    cells = (rows + 2 * REACH) * cols
    taps = 3 * chans
    weight = conv_weight.transpose(0, 3, 1, 2).reshape(taps, taps)
    packed = taps + taps // 2 + 16
    out_t = pair_out.astype(F32).T
    cell_loss, grads = pl.pallas_call(
        functools.partial(tile_kernel, norm=1.0 / (edge * edge)),
        out_shape=(
            jax.ShapeDtypeStruct((rows, cols), F32),
            jax.ShapeDtypeStruct((packed, 2 * chans), F32),
        ),
        in_specs=[vmem] * 7 + [pl.BlockSpec(memory_space=pltpu.HBM)],
        out_specs=(vmem,) * 2,
        scratch_shapes=[
            pltpu.VMEM(target.shape, BF16),
            pltpu.SemaphoreType.DMA,
            pltpu.VMEM((taps, cells), BF16),
            pltpu.VMEM((taps, cells), BF16),
            pltpu.VMEM((rows // 2, chans, 2 * cols), F32),
            pltpu.VMEM((4 * cols, wide), F32),
            pltpu.VMEM((chans, 2 * cols), F32),
            pltpu.VMEM((chans, 2 * cols), F32),
            pltpu.VMEM((chans, 2 * cols), F32),
        ],
        compiler_params=pltpu.CompilerParams(vmem_limit_bytes=40 * 1024 * 1024),
        name="tile",
    )(
        row_sum, col_sum, misc, jnp.concatenate([out_t, out_t], axis=1), pair_bias[:, None], weight,
        conv_bias[:, None], target,
    )

    piece = packed // n_rep
    mine = lax.dynamic_slice_in_dim(grads, rep * piece, piece, 0)
    total = mine + swap(lax.dynamic_slice_in_dim(grads, (1 - rep) * piece, piece, 0), rep=1)
    corner = swap(total, row=1, col=1)
    beside = swap(total, col=1)
    total = (total + beside) + (swap(total, row=1) + corner)
    for step in steps("col", 2):
        total = total + swap(total, col=step)
    for step in steps("row", 2):
        total = total + swap(total, row=step)
    other = swap(total, rep=1)
    grads = jnp.concatenate([jnp.where(rep == 0, total, other), jnp.where(rep == 0, other, total)], axis=0)
    main = grads[:taps].reshape(3, chans, 2, chans).transpose(2, 0, 1, 3)
    last = grads[taps:taps + taps // 2]
    last = jnp.concatenate([last[:, :chans], last[:, chans:]], axis=0).reshape(1, 3, chans, chans)
    grad_conv = jnp.concatenate([main, last], axis=0)
    grad_bias = grads[taps + taps // 2, :chans]
    return cell_loss, grad_conv, grad_bias


def solution(mesh):
    in_specs = (
        P(("grp", "row", "rep"), "col"),
        P(("grp", "col"), "row"),
        P(),
        P(),
        P(),
        P(),
        P(),
        P(),
        P(None, ("grp", "row", "rep"), "col"),
        P(("grp", "row", "rep"), "col"),
    )
    out_specs = (P(("grp", "row", "rep"), "col"), P("grp", None, None, None), P("grp"))
    return jax.shard_map(
        per_device, mesh=mesh, in_specs=in_specs, out_specs=out_specs, check_vma=False
    )
```

```python
import functools

import jax
import jax.numpy as jnp
from jax import lax
from jax.experimental import pallas as pl
from jax.experimental.pallas import tpu as pltpu
from jax.sharding import PartitionSpec as P

REACH = 2
F32 = jnp.float32
BF16 = jnp.bfloat16
ROWS_BY_COLS = (((1,), (1,)), ((), ()))
MESH = ("row", "col", "rep")


def swap(x, row=0, col=0, rep=0):
    sizes = [lax.axis_size(axis) for axis in MESH]

    def index(r, c, p):
        return (r * sizes[1] + c) * sizes[2] + p

    places = [(r, c, p) for r in range(sizes[0]) for c in range(sizes[1]) for p in range(sizes[2])]
    return lax.ppermute(
        x, MESH, [(index(r, c, p), index(r ^ row, c ^ col, p ^ rep)) for r, c, p in places]
    )


def steps(axis, first=1):
    step = first
    while step < lax.axis_size(axis):
        yield step
        step *= 2


def zeros_kernel(zeros_ref):
    zeros_ref[...] = jnp.zeros_like(zeros_ref)


def project_kernel(
    zeros_ref, kept_ref, row_ref, row_proj_ref, col_ref, col_proj_ref,
    col_send_ref, row_send_ref, cross_send_ref, col_wide, *, sliced
):
    row_at = col_at = 0
    depth = row_ref.shape[1]
    if sliced[0]:
        row_at = pl.multiple_of(lax.axis_index("col") * depth, 128)
    if sliced[1]:
        col_at = pl.multiple_of(lax.axis_index("row") * col_ref.shape[0], 16)
    col_wide[...] = jnp.zeros_like(col_wide)
    col_wide[pl.ds(col_at, col_ref.shape[0]), :] = col_ref[...]
    half, wide = row_ref.shape[0] // 2, 2 * row_proj_ref.shape[0]
    lane = lax.broadcasted_iota(jnp.int32, (REACH, wide), 1)

    def packed(x):
        return jnp.concatenate([x[:half], x[half:]], axis=1)

    def ends(x):
        return jnp.where(lane < wide // 2, x[:REACH], x[half - REACH:])

    kept = jnp.broadcast_to(kept_ref[...].astype(F32), (1, wide))
    rows = packed(
        lax.dot_general(
            row_ref[...], row_proj_ref[:, pl.ds(row_at, depth)], ROWS_BY_COLS, preferred_element_type=F32
        )
    )
    cols = packed(jnp.dot(col_proj_ref[...], col_wide[...], preferred_element_type=F32).T)
    row_ends, col_ends = ends(rows), ends(cols)
    zero = zeros_ref[...]
    col_send_ref[0:half, :] = rows
    row_send_ref[0:half, :] = cols
    col_send_ref[half:, :] = jnp.concatenate([col_ends, kept, zero[:5]], axis=0)
    row_send_ref[half:, :] = jnp.concatenate([row_ends, kept, zero[:5]], axis=0)
    cross_send_ref[...] = jnp.concatenate([row_ends, kept, col_ends, zero[:3]], axis=0)


def tile_kernel(
    row_ref, col_ref, misc_ref, out_ref, pbias_ref, weight_ref, cbias_ref, target_ref,
    loss_ref, grad_ref, hid, dif_taps, feat, rhs, turned_target, *, norm
):
    chans, rows, cols = target_ref.shape
    half, wide = row_ref.shape
    rank = wide // 2
    width = 2 * cols
    pairs = rows // 2 + 2
    taps = weight_ref.shape[0]

    kept = misc_ref[4:5, 0:1]
    lane = lax.broadcasted_iota(jnp.int32, (half, wide), 1)
    rhs[...] = jnp.zeros_like(rhs)
    after_map, before_map = misc_ref[5:6, 0:1], misc_ref[5:6, wide - 1:wide]
    one = jnp.ones((1, 1), F32)
    pieces = ((0, col_ref[...], half, kept, kept), (cols, misc_ref[0:REACH, :], cols - REACH, after_map, before_map))
    for start, value, gap, mask_first, mask_last in pieces:
        turned = pltpu.roll(value, rank, 1)
        size = value.shape[0]
        lower = lane[:size] < rank
        for base, first, last in ((0, value, turned), (2 * cols, turned, value)):
            keep_half = lower if base == 0 else ~lower
            at = base + start
            for x, mask in ((first, mask_first), (last, mask_last)):
                x = jnp.where(keep_half, x, 0.0)
                for plane, factor in enumerate((mask, one)):
                    rhs[plane, at:at + size, :wide] = x * factor
                    rhs[plane, at:at + size, wide:] = jnp.where(lane[:size] < 3, factor, 0.0)
                at += gap
    factors = [rhs[plane].astype(BF16) for plane in range(2)]

    lane = lax.broadcasted_iota(jnp.int32, (chans, cols), 1)
    pair_out = out_ref[...]
    high = pbias_ref[...].astype(BF16).astype(F32)
    rest = pbias_ref[...] - high
    middle = rest.astype(BF16).astype(F32)
    bias_parts = jnp.where(
        lane == 0, high, jnp.where(lane == 1, middle, jnp.where(lane == 2, rest - middle, 0.0))
    ).astype(BF16)
    last_two, first_two = lane >= cols - REACH, lane < REACH

    def features(rounded, places, plane):
        scaled = jnp.concatenate([pair_out * rounded[j:j + 1] for j in range(len(places))], axis=0)
        scaled = jnp.concatenate(
            [scaled.astype(BF16), jnp.concatenate([bias_parts] * len(places), axis=0)], axis=1
        )
        values = lax.dot_general(scaled, factors[plane], ROWS_BY_COLS, preferred_element_type=F32)
        for j, place in enumerate(places):
            for side, i in enumerate(place):
                value = values[j * chans:(j + 1) * chans, side * width:(side + 1) * width]
                own, beside = value[:, :cols], value[:, cols:]
                if plane == 0:
                    feat[i // 2, :, (i % 2) * cols:(i % 2 + 1) * cols] = own
                else:
                    zone = 6 if i < 0 else 8
                    own = own * misc_ref[zone:zone + 1, :]
                    beside = beside * misc_ref[zone + 1:zone + 2, :]
                own, beside = (jnp.maximum(x.astype(BF16), 0) for x in (own, beside))
                before = pltpu.roll(jnp.where(last_two, beside, own), REACH, 1)
                after = pltpu.roll(jnp.where(first_two, beside, own), cols - REACH, 1)
                at = slice((i + REACH) * cols, (i + REACH + 1) * cols)
                hid[0:chans, at] = before.astype(BF16)
                hid[chans:2 * chans, at] = own.astype(BF16)
                hid[2 * chans:3 * chans, at] = after.astype(BF16)

    def rounded(x):
        return x.astype(BF16).astype(F32)

    features(rounded(misc_ref[REACH:2 * REACH, :]), [(rows + j, j - REACH) for j in range(REACH)], 1)
    for m in range(0, half, GROUP):
        features(rounded(row_ref[m:m + GROUP, :]), [(m + j, half + m + j) for j in range(GROUP)], 0)
        if (2 * m) % 16 == 0:
            turned_target[2 * m:2 * m + 16] = jnp.swapaxes(target_ref[:, 2 * m:2 * m + 16, :], 0, 1)

    zero = jnp.zeros((chans, width), BF16)
    for tap, e in ((0, pairs - 2), (0, pairs - 1), (1, 0), (1, pairs - 1), (2, 0), (2, 1)):
        dif_taps[tap * chans:(tap + 1) * chans, e * width:(e + 1) * width] = zero
    cbias = jnp.broadcast_to(cbias_ref[...], (chans, width))
    keep = jnp.concatenate([misc_ref[4:5, :]] * 2, axis=1)
    bias_sum = jnp.zeros((chans, width), F32)
    for e in range(pairs):
        part = jnp.dot(weight_ref[...], hid[:, e * width:(e + 1) * width], preferred_element_type=F32)
        m = e - 2
        if m >= 0:
            target = jnp.concatenate([turned_target[2 * m], turned_target[2 * m + 1]], axis=1).astype(F32)
            out = near + part[2 * chans:]
            differ = keep * (feat[m] + (out + cbias) - target)
            loss = 0.5 * jnp.sum(differ * differ, axis=0, keepdims=True)
            loss_ref[2 * m:2 * m + 1, :] = loss[:, :cols]
            loss_ref[2 * m + 1:2 * m + 2, :] = loss[:, cols:]
            bias_sum = bias_sum + differ
            grad_in = differ.astype(BF16)
            for tap in range(3):
                dif_taps[tap * chans:(tap + 1) * chans, (m + tap) * width:(m + tap + 1) * width] = grad_in
        if e > 0:
            near = far + part[chans:2 * chans]
        far = part[0:chans]

    grad = lax.dot_general(hid[...], dif_taps[...], ROWS_BY_COLS, preferred_element_type=F32) * norm
    split = taps // 2
    grad_ref[0:taps, :] = grad[:, 0:2 * chans]
    last = grad[:, 2 * chans:]
    grad_ref[taps:taps + split, :] = jnp.concatenate([last[:split], last[split:]], axis=1)
    sums = bias_sum[:, :cols] + bias_sum[:, cols:]
    bias = lax.dot_general(
        jnp.ones((8, cols), F32), sums, ROWS_BY_COLS, preferred_element_type=F32, precision=lax.Precision.HIGHEST
    )
    grad_ref[taps + split:, :] = jnp.zeros((grad_ref.shape[0] - taps - split, 2 * chans), F32)
    grad_ref[taps + split:taps + split + 8, 0:chans] = bias * norm


def unpack_kernel(own_ref, other_ref, conv_ref, bias_ref):
    chans = conv_ref.shape[3]
    first = lax.axis_index("rep") == 0
    own, other = own_ref[...], other_ref[...]
    whole = jnp.concatenate([jnp.where(first, own, other), jnp.where(first, other, own)], axis=0)
    taps, split = 3 * chans, 3 * chans // 2
    for a in range(2):
        for b in range(3):
            conv_ref[a, b] = whole[b * chans:(b + 1) * chans, a * chans:(a + 1) * chans]
    last = jnp.concatenate([whole[taps:taps + split, :chans], whole[taps:taps + split, chans:]], axis=0)
    for b in range(3):
        conv_ref[2, b] = last[b * chans:(b + 1) * chans]
    bias_ref[...] = whole[taps + split:taps + split + 1, :chans]


GROUP = 4


def per_device(
    emb_row, emb_col, proj_row, proj_col, pair_out, pair_bias, conv_weight, conv_bias, target, kept_tiles
):
    chans, rows, cols = target.shape
    rank = pair_out.shape[0]
    row, col, rep = (lax.axis_index(axis) for axis in MESH)
    n_row, n_col, n_rep = (lax.axis_size(axis) for axis in MESH)
    edge = rows // kept_tiles.shape[0]
    half, wide = rows // 2, 2 * rank
    vmem = pl.BlockSpec(memory_space=pltpu.VMEM)

    shares = emb_row.shape[1], emb_col.shape[1]
    sliced = (shares[0] % 128 == 0, shares[1] % 16 == 0)
    projs = [proj_row.T, proj_col.T]
    for side, place in enumerate((col, row)):
        if not sliced[side]:
            projs[side] = lax.dynamic_slice_in_dim(projs[side], place * shares[side], shares[side], 1)
    zeros = pl.pallas_call(
        zeros_kernel,
        out_shape=jax.ShapeDtypeStruct((8, wide), F32),
        out_specs=vmem,
        compiler_params=pltpu.CompilerParams(vmem_limit_bytes=4 * 1024 * 1024),
        cost_estimate=pl.CostEstimate(flops=4 * 10**9, bytes_accessed=1000, transcendentals=0),
        name="zeros",
    )()
    col_send, row_send, cross_send = pl.pallas_call(
        functools.partial(project_kernel, sliced=sliced),
        out_shape=(
            jax.ShapeDtypeStruct((half + 8, wide), F32),
            jax.ShapeDtypeStruct((half + 8, wide), F32),
            jax.ShapeDtypeStruct((8, wide), F32),
        ),
        in_specs=[vmem] * 6,
        out_specs=(vmem,) * 3,
        scratch_shapes=[pltpu.VMEM((projs[1].shape[1], cols), BF16)],
        compiler_params=pltpu.CompilerParams(vmem_limit_bytes=4 * 1024 * 1024),
        cost_estimate=pl.CostEstimate(flops=2 * 10**9, bytes_accessed=1000, transcendentals=0),
        name="project",
    )(zeros, kept_tiles, emb_row, projs[0], emb_col.T, projs[1])

    shift = [[(i, (i + k) % n_col) for i in range(n_col)] for k in range(n_col)]
    row_cols = ("row", "col", "rep")

    def cross(x, k):
        def index(r, c, p):
            return (r * n_col + c) * n_rep + p

        return lax.ppermute(
            x, row_cols,
            [
                (index(r, c, p), index(r ^ 1, (c + k) % n_col, p ^ 1))
                for r in range(n_row) for c in range(n_col) for p in range(n_rep)
            ],
        )

    from_cross = {k: cross(cross_send, k) for k in range(1, n_col)}
    from_col = {k: lax.ppermute(col_send, "col", shift[k]) for k in range(1, n_col)}
    from_row = swap(row_send, row=1, rep=1)

    lane = lax.broadcasted_iota(jnp.int32, (1, wide), 1)
    lower = lane < rank

    def sides(blocks, at, size):
        return jnp.where(lower, blocks[n_col - 1][at:at + size], blocks[1][at:at + size])

    def outside(mask):
        return jnp.where(jnp.where(lower, col < n_col - 1, col > 0), mask, 0.0)

    row_sum = col_send[:half] + sum(from_col[k][:half] for k in from_col)
    col_sum = row_send[:half] + from_row[:half]
    side = sides(from_col, half, REACH) + sides(from_cross, REACH + 1, REACH)
    own_kept = col_send[half + REACH:half + REACH + 1]
    own_masks = jnp.concatenate([own_kept, outside(sides(from_col, half + REACH, 1))], axis=0)
    own_ends = jnp.where(lower, row_sum[:REACH], row_sum[half - REACH:])
    block = jnp.concatenate(
        [
            from_row[half:half + REACH] + sum(from_cross[k][:REACH] for k in from_cross),
            from_row[half + REACH:half + REACH + 1],
            outside(sides(from_cross, REACH, 1)),
        ],
        axis=0,
    )
    mate = swap(jnp.concatenate([own_ends, own_masks, jnp.zeros((4, wide), F32)], axis=0), rep=1)

    blocks = {1: block}
    pad = jnp.zeros((2, wide), F32)
    for step in steps("row", 2):
        got = swap(jnp.concatenate([col_sum, side, blocks[step - 1], pad], axis=0), row=step)
        col_sum = col_sum + got[:half]
        side = side + got[half:half + REACH]
        blocks[2 * step - 1] = got[half + REACH:half + REACH + 4]

    beyond = jnp.where(rep == 0, row - 1, row + 1)
    far = blocks[1]
    for apart, found in blocks.items():
        far = jnp.where((row ^ beyond) == apart, found, far)
    far_masks = jnp.where((beyond >= 0) & (beyond < n_row), far[REACH:], 0.0)
    above = jnp.where(rep == 0, far[:REACH], mate[:REACH])
    below = jnp.where(rep == 0, mate[:REACH], far[:REACH])
    mate_masks = mate[REACH:REACH + 2]
    misc = jnp.concatenate(
        [
            side,
            jnp.where(lower, below, above),
            own_masks,
            jnp.where(rep == 0, far_masks, mate_masks),
            jnp.where(rep == 0, mate_masks, far_masks),
            jnp.zeros((6, wide), F32),
        ],
        axis=0,
    )

    cells = (rows + 2 * REACH) * cols
    taps = 3 * chans
    weight = conv_weight.transpose(0, 3, 1, 2).reshape(taps, taps)
    packed = taps + taps // 2 + 16
    out_t = pair_out.astype(F32).T
    cell_loss, grads = pl.pallas_call(
        functools.partial(tile_kernel, norm=1.0 / (edge * edge)),
        out_shape=(
            jax.ShapeDtypeStruct((rows, cols), F32),
            jax.ShapeDtypeStruct((packed, 2 * chans), F32),
        ),
        in_specs=[vmem] * 8,
        out_specs=(vmem,) * 2,
        scratch_shapes=[
            pltpu.VMEM((taps, cells), BF16),
            pltpu.VMEM((taps, cells), BF16),
            pltpu.VMEM((rows // 2, chans, 2 * cols), F32),
            pltpu.VMEM((2, 4 * cols, 2 * wide), F32),
            pltpu.VMEM((rows, chans, cols), BF16),
        ],
        compiler_params=pltpu.CompilerParams(vmem_limit_bytes=40 * 1024 * 1024),
        name="tile",
    )(
        row_sum, col_sum, misc, jnp.concatenate([out_t, out_t], axis=1), pair_bias[:, None], weight,
        conv_bias[:, None], target,
    )

    piece = packed // n_rep
    mine = lax.dynamic_slice_in_dim(grads, rep * piece, piece, 0)
    total = mine + swap(lax.dynamic_slice_in_dim(grads, (1 - rep) * piece, piece, 0), rep=1)
    corner = swap(total, row=1, col=1)
    beside = swap(total, col=1)
    total = (total + beside) + (swap(total, row=1) + corner)
    for step in steps("col", 2):
        total = total + swap(total, col=step)
    for step in steps("row", 2):
        total = total + swap(total, row=step)
    other = swap(total, rep=1)
    grad_conv, grad_bias = pl.pallas_call(
        unpack_kernel,
        out_shape=(jax.ShapeDtypeStruct((3, 3, chans, chans), F32), jax.ShapeDtypeStruct((1, chans), F32)),
        in_specs=[vmem] * 2,
        out_specs=(vmem,) * 2,
        compiler_params=pltpu.CompilerParams(vmem_limit_bytes=4 * 1024 * 1024),
        name="unpack",
    )(total, other)
    return cell_loss, grad_conv, grad_bias[0]


def solution(mesh):
    in_specs = (
        P(("grp", "row", "rep"), "col"),
        P(("grp", "col"), "row"),
        P(),
        P(),
        P(),
        P(),
        P(),
        P(),
        P(None, ("grp", "row", "rep"), "col"),
        P(("grp", "row", "rep"), "col"),
    )
    out_specs = (P(("grp", "row", "rep"), "col"), P("grp", None, None, None), P("grp"))
    return jax.shard_map(
        per_device, mesh=mesh, in_specs=in_specs, out_specs=out_specs, check_vma=False
    )
```

```python
import functools

import jax
import jax.numpy as jnp
from jax import lax
from jax.experimental import pallas as pl
from jax.experimental.pallas import tpu as pltpu
from jax.sharding import PartitionSpec as P

REACH = 2
F32 = jnp.float32
BF16 = jnp.bfloat16
ROWS_BY_COLS = (((1,), (1,)), ((), ()))
MESH = ("row", "col", "rep")


def send(x, target):
    sizes = [lax.axis_size(axis) for axis in MESH]

    def index(r, c, p):
        return (r * sizes[1] + c) * sizes[2] + p

    places = [(r, c, p) for r in range(sizes[0]) for c in range(sizes[1]) for p in range(sizes[2])]
    return lax.ppermute(x, MESH, [(index(*place), index(*target(*place))) for place in places])


def swap(x, row=0, col=0, rep=0):
    return send(x, lambda r, c, p: (r ^ row, c ^ col, p ^ rep))


def steps(axis, first=1):
    step = first
    while step < lax.axis_size(axis):
        yield step
        step *= 2


def zeros_kernel(zeros_ref):
    zeros_ref[...] = jnp.zeros_like(zeros_ref)


def project_kernel(
    zeros_ref, kept_ref, row_ref, row_proj_ref, col_ref, col_proj_ref,
    col_send_ref, row_send_ref, ends_send_ref, col_wide, *, sliced
):
    row_at = col_at = 0
    depth = row_ref.shape[1]
    if sliced[0]:
        row_at = pl.multiple_of(lax.axis_index("col") * depth, 128)
    if sliced[1]:
        col_at = pl.multiple_of(lax.axis_index("row") * col_ref.shape[0], 16)
    col_wide[...] = jnp.zeros_like(col_wide)
    col_wide[pl.ds(col_at, col_ref.shape[0]), :] = col_ref[...]
    half, wide = row_ref.shape[0] // 2, 2 * row_proj_ref.shape[0]
    lane = lax.broadcasted_iota(jnp.int32, (REACH, wide), 1)

    def packed(x):
        return jnp.concatenate([x[:half], x[half:]], axis=1)

    def ends(x):
        return jnp.where(lane < wide // 2, x[:REACH], x[half - REACH:])

    kept = jnp.broadcast_to(kept_ref[...].astype(F32), (1, wide))
    rows = packed(
        lax.dot_general(
            row_ref[...], row_proj_ref[:, pl.ds(row_at, depth)], ROWS_BY_COLS, preferred_element_type=F32
        )
    )
    cols = packed(jnp.dot(col_proj_ref[...], col_wide[...], preferred_element_type=F32).T)
    row_ends, col_ends = ends(rows), ends(cols)
    zero = zeros_ref[...]
    col_send_ref[0:half, :] = rows
    row_send_ref[0:half, :] = cols
    col_send_ref[half:, :] = jnp.concatenate([kept, zero[:7]], axis=0)
    row_send_ref[half:, :] = jnp.concatenate([row_ends, kept, zero[:5]], axis=0)
    ends_send_ref[...] = jnp.concatenate([row_ends, kept, col_ends, zero[:3]], axis=0)


def tile_kernel(
    row_ref, col_ref, misc_ref, out_ref, pbias_ref, weight_ref, cbias_ref, target_ref,
    loss_ref, grad_ref, hid, dif_taps, feat, rhs, turned_target, *, norm
):
    chans, rows, cols = target_ref.shape
    half, wide = row_ref.shape
    rank = wide // 2
    width = 2 * cols
    pairs = rows // 2 + 2
    taps = weight_ref.shape[0]

    kept = misc_ref[4:5, 0:1]
    lane = lax.broadcasted_iota(jnp.int32, (half, wide), 1)
    rhs[...] = jnp.zeros_like(rhs)
    after_map, before_map = misc_ref[5:6, 0:1], misc_ref[5:6, wide - 1:wide]
    one = jnp.ones((1, 1), F32)
    pieces = ((0, col_ref[...], half, kept, kept), (cols, misc_ref[0:REACH, :], cols - REACH, after_map, before_map))
    for start, value, gap, mask_first, mask_last in pieces:
        turned = pltpu.roll(value, rank, 1)
        size = value.shape[0]
        lower = lane[:size] < rank
        for base, first, last in ((0, value, turned), (2 * cols, turned, value)):
            keep_half = lower if base == 0 else ~lower
            at = base + start
            for x, mask in ((first, mask_first), (last, mask_last)):
                x = jnp.where(keep_half, x, 0.0)
                for plane, factor in enumerate((mask, one)):
                    rhs[plane, at:at + size, :wide] = x * factor
                    rhs[plane, at:at + size, wide:] = jnp.where(lane[:size] < 3, factor, 0.0)
                at += gap
    factors = [rhs[plane].astype(BF16) for plane in range(2)]

    lane = lax.broadcasted_iota(jnp.int32, (chans, cols), 1)
    pair_out = out_ref[...]
    high = pbias_ref[...].astype(BF16).astype(F32)
    rest = pbias_ref[...] - high
    middle = rest.astype(BF16).astype(F32)
    bias_parts = jnp.where(
        lane == 0, high, jnp.where(lane == 1, middle, jnp.where(lane == 2, rest - middle, 0.0))
    ).astype(BF16)
    last_two, first_two = lane >= cols - REACH, lane < REACH

    def features(rounded, places, plane):
        scaled = jnp.concatenate([pair_out * rounded[j:j + 1] for j in range(len(places))], axis=0)
        scaled = jnp.concatenate(
            [scaled.astype(BF16), jnp.concatenate([bias_parts] * len(places), axis=0)], axis=1
        )
        values = lax.dot_general(scaled, factors[plane], ROWS_BY_COLS, preferred_element_type=F32)
        for j, place in enumerate(places):
            for side, i in enumerate(place):
                value = values[j * chans:(j + 1) * chans, side * width:(side + 1) * width]
                own, beside = value[:, :cols], value[:, cols:]
                if plane == 0:
                    feat[i // 2, :, (i % 2) * cols:(i % 2 + 1) * cols] = own
                else:
                    zone = 6 if i < 0 else 8
                    own = own * misc_ref[zone:zone + 1, :]
                    beside = beside * misc_ref[zone + 1:zone + 2, :]
                own, beside = (jnp.maximum(x.astype(BF16), 0) for x in (own, beside))
                before = pltpu.roll(jnp.where(last_two, beside, own), REACH, 1)
                after = pltpu.roll(jnp.where(first_two, beside, own), cols - REACH, 1)
                at = slice((i + REACH) * cols, (i + REACH + 1) * cols)
                hid[0:chans, at] = before.astype(BF16)
                hid[chans:2 * chans, at] = own.astype(BF16)
                hid[2 * chans:3 * chans, at] = after.astype(BF16)

    def rounded(x):
        return x.astype(BF16).astype(F32)

    features(rounded(misc_ref[REACH:2 * REACH, :]), [(rows + j, j - REACH) for j in range(REACH)], 1)
    for m in range(0, half, GROUP):
        features(rounded(row_ref[m:m + GROUP, :]), [(m + j, half + m + j) for j in range(GROUP)], 0)
        if (2 * m) % 16 == 0:
            turned_target[2 * m:2 * m + 16] = jnp.swapaxes(target_ref[:, 2 * m:2 * m + 16, :], 0, 1)

    zero = jnp.zeros((chans, width), BF16)
    for tap, e in ((0, pairs - 2), (0, pairs - 1), (1, 0), (1, pairs - 1), (2, 0), (2, 1)):
        dif_taps[tap * chans:(tap + 1) * chans, e * width:(e + 1) * width] = zero
    cbias = jnp.broadcast_to(cbias_ref[...], (chans, width))
    keep = jnp.concatenate([misc_ref[4:5, :]] * 2, axis=1)
    bias_sum = jnp.zeros((chans, width), F32)
    for e in range(pairs):
        part = jnp.dot(weight_ref[...], hid[:, e * width:(e + 1) * width], preferred_element_type=F32)
        m = e - 2
        if m >= 0:
            target = jnp.concatenate([turned_target[2 * m], turned_target[2 * m + 1]], axis=1).astype(F32)
            out = near + part[2 * chans:]
            differ = keep * (feat[m] + (out + cbias) - target)
            loss = 0.5 * jnp.sum(differ * differ, axis=0, keepdims=True)
            loss_ref[2 * m:2 * m + 1, :] = loss[:, :cols]
            loss_ref[2 * m + 1:2 * m + 2, :] = loss[:, cols:]
            bias_sum = bias_sum + differ
            grad_in = differ.astype(BF16)
            for tap in range(3):
                dif_taps[tap * chans:(tap + 1) * chans, (m + tap) * width:(m + tap + 1) * width] = grad_in
        if e > 0:
            near = far + part[chans:2 * chans]
        far = part[0:chans]

    grad = lax.dot_general(hid[...], dif_taps[...], ROWS_BY_COLS, preferred_element_type=F32) * norm
    split = taps // 2
    grad_ref[0:taps, :] = grad[:, 0:2 * chans]
    last = grad[:, 2 * chans:]
    grad_ref[taps:taps + split, :] = jnp.concatenate([last[:split], last[split:]], axis=1)
    sums = bias_sum[:, :cols] + bias_sum[:, cols:]
    bias = lax.dot_general(
        jnp.ones((8, cols), F32), sums, ROWS_BY_COLS, preferred_element_type=F32, precision=lax.Precision.HIGHEST
    )
    grad_ref[taps + split:, :] = jnp.zeros((grad_ref.shape[0] - taps - split, 2 * chans), F32)
    grad_ref[taps + split:taps + split + 8, 0:chans] = bias * norm


def unpack_kernel(own_ref, other_ref, conv_ref, bias_ref):
    chans = conv_ref.shape[3]
    first = lax.axis_index("rep") == 0
    own, other = own_ref[...], other_ref[...]
    whole = jnp.concatenate([jnp.where(first, own, other), jnp.where(first, other, own)], axis=0)
    taps, split = 3 * chans, 3 * chans // 2
    for a in range(2):
        for b in range(3):
            conv_ref[a, b] = whole[b * chans:(b + 1) * chans, a * chans:(a + 1) * chans]
    last = jnp.concatenate([whole[taps:taps + split, :chans], whole[taps:taps + split, chans:]], axis=0)
    for b in range(3):
        conv_ref[2, b] = last[b * chans:(b + 1) * chans]
    bias_ref[...] = whole[taps + split:taps + split + 1, :chans]


GROUP = 4


def per_device(
    emb_row, emb_col, proj_row, proj_col, pair_out, pair_bias, conv_weight, conv_bias, target, kept_tiles
):
    chans, rows, cols = target.shape
    rank = pair_out.shape[0]
    row, col, rep = (lax.axis_index(axis) for axis in MESH)
    n_row, n_col, n_rep = (lax.axis_size(axis) for axis in MESH)
    edge = rows // kept_tiles.shape[0]
    half, wide = rows // 2, 2 * rank
    vmem = pl.BlockSpec(memory_space=pltpu.VMEM)

    shares = emb_row.shape[1], emb_col.shape[1]
    sliced = (shares[0] % 128 == 0, shares[1] % 16 == 0)
    projs = [proj_row.T, proj_col.T]
    for side, place in enumerate((col, row)):
        if not sliced[side]:
            projs[side] = lax.dynamic_slice_in_dim(projs[side], place * shares[side], shares[side], 1)
    zeros = pl.pallas_call(
        zeros_kernel,
        out_shape=jax.ShapeDtypeStruct((8, wide), F32),
        out_specs=vmem,
        compiler_params=pltpu.CompilerParams(vmem_limit_bytes=4 * 1024 * 1024),
        cost_estimate=pl.CostEstimate(flops=4 * 10**9, bytes_accessed=1000, transcendentals=0),
        name="zeros",
    )()
    col_send, row_send, ends_send = pl.pallas_call(
        functools.partial(project_kernel, sliced=sliced),
        out_shape=(
            jax.ShapeDtypeStruct((half + 8, wide), F32),
            jax.ShapeDtypeStruct((half + 8, wide), F32),
            jax.ShapeDtypeStruct((8, wide), F32),
        ),
        in_specs=[vmem] * 6,
        out_specs=(vmem,) * 3,
        scratch_shapes=[pltpu.VMEM((projs[1].shape[1], cols), BF16)],
        compiler_params=pltpu.CompilerParams(vmem_limit_bytes=4 * 1024 * 1024),
        cost_estimate=pl.CostEstimate(flops=2 * 10**9, bytes_accessed=1000, transcendentals=0),
        name="project",
    )(zeros, kept_tiles, emb_row, projs[0], emb_col.T, projs[1])

    def shifted(x, k, row, rep):
        return send(x, lambda r, c, p: (r ^ row, (c + k) % n_col, p ^ rep))

    from_cross = {k: shifted(ends_send, k, 1, 0) for k in range(1, n_col)}
    from_mates = {k: shifted(ends_send, k, 0, 1) for k in range(1, n_col)}
    from_row = swap(row_send, row=1)

    lane = lax.broadcasted_iota(jnp.int32, (1, wide), 1)
    lower = lane < rank

    def sides(blocks, at, size):
        return jnp.where(lower, blocks[n_col - 1][at:at + size], blocks[1][at:at + size])

    def masks(kept, blocks, at):
        beside = jnp.where(jnp.where(lower, col < n_col - 1, col > 0), sides(blocks, at, 1), 0.0)
        return jnp.concatenate([kept, beside], axis=0)

    col_sum = row_send[:half] + from_row[:half]
    side = sides(from_mates, REACH + 1, REACH) + sides(from_cross, REACH + 1, REACH)
    block = jnp.concatenate(
        [
            from_row[half:half + REACH] + sum(from_cross[k][:REACH] for k in from_cross),
            masks(from_row[half + REACH:half + REACH + 1], from_cross, REACH),
        ],
        axis=0,
    )

    from_col = {k: shifted(col_send, k, 0, 0) for k in range(1, n_col)}
    row_sum = col_send[:half] + sum(from_col[k][:half] for k in from_col)
    own_masks = masks(col_send[half:half + 1], from_col, half)

    mate = swap(jnp.concatenate([ends_send[:REACH + 2], block], axis=0), rep=1)
    mate_ends = mate[:REACH] + sum(from_mates[k][:REACH] for k in from_mates)
    mate_masks = masks(mate[REACH:REACH + 1], from_mates, REACH)

    blocks = {1: mate[REACH + 2:]}
    pad = jnp.zeros((2, wide), F32)
    for step in steps("row", 2):
        got = swap(jnp.concatenate([col_sum, side, block, pad], axis=0), row=step, rep=1 if step == 2 else 0)
        col_sum = col_sum + got[:half]
        side = side + got[half:half + REACH]
        block = got[half + REACH:half + REACH + 4]
        blocks[2 * step - 1] = block

    beyond = jnp.where(rep == 0, row - 1, row + 1)
    far = blocks[1]
    for apart, found in blocks.items():
        far = jnp.where((row ^ beyond) == apart, found, far)
    far_masks = jnp.where((beyond >= 0) & (beyond < n_row), far[REACH:], 0.0)
    above = jnp.where(rep == 0, far[:REACH], mate_ends)
    below = jnp.where(rep == 0, mate_ends, far[:REACH])
    misc = jnp.concatenate(
        [
            side,
            jnp.where(lower, below, above),
            own_masks,
            jnp.where(rep == 0, far_masks, mate_masks),
            jnp.where(rep == 0, mate_masks, far_masks),
            jnp.zeros((6, wide), F32),
        ],
        axis=0,
    )

    cells = (rows + 2 * REACH) * cols
    taps = 3 * chans
    weight = conv_weight.transpose(0, 3, 1, 2).reshape(taps, taps)
    packed = taps + taps // 2 + 16
    out_t = pair_out.astype(F32).T
    cell_loss, grads = pl.pallas_call(
        functools.partial(tile_kernel, norm=1.0 / (edge * edge)),
        out_shape=(
            jax.ShapeDtypeStruct((rows, cols), F32),
            jax.ShapeDtypeStruct((packed, 2 * chans), F32),
        ),
        in_specs=[vmem] * 8,
        out_specs=(vmem,) * 2,
        scratch_shapes=[
            pltpu.VMEM((taps, cells), BF16),
            pltpu.VMEM((taps, cells), BF16),
            pltpu.VMEM((rows // 2, chans, 2 * cols), F32),
            pltpu.VMEM((2, 4 * cols, 2 * wide), F32),
            pltpu.VMEM((rows, chans, cols), BF16),
        ],
        compiler_params=pltpu.CompilerParams(vmem_limit_bytes=40 * 1024 * 1024),
        name="tile",
    )(
        row_sum, col_sum, misc, jnp.concatenate([out_t, out_t], axis=1), pair_bias[:, None], weight,
        conv_bias[:, None], target,
    )

    piece = packed // n_rep
    mine = lax.dynamic_slice_in_dim(grads, rep * piece, piece, 0)
    total = mine + swap(lax.dynamic_slice_in_dim(grads, (1 - rep) * piece, piece, 0), rep=1)
    corner = swap(total, row=1, col=1)
    beside = swap(total, col=1)
    total = (total + beside) + (swap(total, row=1) + corner)
    for step in steps("col", 2):
        total = total + swap(total, col=step)
    for step in steps("row", 2):
        total = total + swap(total, row=step)
    other = swap(total, rep=1)
    grad_conv, grad_bias = pl.pallas_call(
        unpack_kernel,
        out_shape=(jax.ShapeDtypeStruct((3, 3, chans, chans), F32), jax.ShapeDtypeStruct((1, chans), F32)),
        in_specs=[vmem] * 2,
        out_specs=(vmem,) * 2,
        compiler_params=pltpu.CompilerParams(vmem_limit_bytes=4 * 1024 * 1024),
        name="unpack",
    )(total, other)
    return cell_loss, grad_conv, grad_bias[0]


def solution(mesh):
    in_specs = (
        P(("grp", "row", "rep"), "col"),
        P(("grp", "col"), "row"),
        P(),
        P(),
        P(),
        P(),
        P(),
        P(),
        P(None, ("grp", "row", "rep"), "col"),
        P(("grp", "row", "rep"), "col"),
    )
    out_specs = (P(("grp", "row", "rep"), "col"), P("grp", None, None, None), P("grp"))
    return jax.shard_map(
        per_device, mesh=mesh, in_specs=in_specs, out_specs=out_specs, check_vma=False
    )
```

```python
import functools

import jax
import jax.numpy as jnp
from jax import lax
from jax.experimental import pallas as pl
from jax.experimental.pallas import tpu as pltpu
from jax.sharding import PartitionSpec as P

REACH = 2
F32 = jnp.float32
BF16 = jnp.bfloat16
ROWS_BY_COLS = (((1,), (1,)), ((), ()))
MESH = ("row", "col", "rep")


def send(x, target):
    sizes = [lax.axis_size(axis) for axis in MESH]

    def index(r, c, p):
        return (r * sizes[1] + c) * sizes[2] + p

    places = [(r, c, p) for r in range(sizes[0]) for c in range(sizes[1]) for p in range(sizes[2])]
    return lax.ppermute(x, MESH, [(index(*place), index(*target(*place))) for place in places])


def swap(x, row=0, col=0, rep=0):
    return send(x, lambda r, c, p: (r ^ row, c ^ col, p ^ rep))


def steps(axis, first=1):
    step = first
    while step < lax.axis_size(axis):
        yield step
        step *= 2


def zeros_kernel(zeros_ref):
    zeros_ref[...] = jnp.zeros_like(zeros_ref)


def project_kernel(
    zeros_ref, kept_ref, row_ref, row_proj_ref, col_ref, col_proj_ref,
    col_send_ref, row_send_ref, ends_send_ref, col_wide, *, sliced
):
    row_at = col_at = 0
    depth = row_ref.shape[1]
    if sliced[0]:
        row_at = pl.multiple_of(lax.axis_index("col") * depth, 128)
    if sliced[1]:
        col_at = pl.multiple_of(lax.axis_index("row") * col_ref.shape[0], 16)
    col_wide[...] = jnp.zeros_like(col_wide)
    col_wide[pl.ds(col_at, col_ref.shape[0]), :] = col_ref[...]
    half, wide = row_ref.shape[0] // 2, 2 * row_proj_ref.shape[0]
    lane = lax.broadcasted_iota(jnp.int32, (REACH, wide), 1)

    def packed(x):
        return jnp.concatenate([x[:half], x[half:]], axis=1)

    def ends(x):
        return jnp.where(lane < wide // 2, x[:REACH], x[half - REACH:])

    kept = jnp.broadcast_to(kept_ref[...].astype(F32), (1, wide))
    rows = packed(
        lax.dot_general(
            row_ref[...], row_proj_ref[:, pl.ds(row_at, depth)], ROWS_BY_COLS, preferred_element_type=F32
        )
    )
    cols = packed(jnp.dot(col_proj_ref[...], col_wide[...], preferred_element_type=F32).T)
    row_ends, col_ends = ends(rows), ends(cols)
    zero = zeros_ref[...]
    col_send_ref[0:half, :] = rows
    row_send_ref[0:half, :] = cols
    col_send_ref[half:, :] = jnp.concatenate([kept, zero[:7]], axis=0)
    row_send_ref[half:, :] = jnp.concatenate([row_ends, kept, zero[:5]], axis=0)
    ends_send_ref[...] = jnp.concatenate([row_ends, kept, col_ends, zero[:3]], axis=0)


def tile_kernel(
    row_ref, col_ref, misc_ref, out_ref, pbias_ref, weight_ref, cbias_ref, target_ref,
    loss_ref, grad_ref, hid, dif_taps, feat, rhs, turned_target, *, norm
):
    chans, rows, cols = target_ref.shape
    half, wide = row_ref.shape
    rank = wide // 2
    width = 2 * cols
    pairs = rows // 2 + 2
    taps = weight_ref.shape[0]

    kept = misc_ref[4:5, 0:1]
    lane = lax.broadcasted_iota(jnp.int32, (half, wide), 1)
    rhs[...] = jnp.zeros_like(rhs)
    after_map, before_map = misc_ref[5:6, 0:1], misc_ref[5:6, wide - 1:wide]
    one = jnp.ones((1, 1), F32)
    pieces = ((0, col_ref[...], half, kept, kept), (cols, misc_ref[0:REACH, :], cols - REACH, after_map, before_map))
    for start, value, gap, mask_first, mask_last in pieces:
        turned = pltpu.roll(value, rank, 1)
        size = value.shape[0]
        lower = lane[:size] < rank
        for base, first, last in ((0, value, turned), (2 * cols, turned, value)):
            keep_half = lower if base == 0 else ~lower
            at = base + start
            for x, mask in ((first, mask_first), (last, mask_last)):
                x = jnp.where(keep_half, x, 0.0)
                for plane, factor in enumerate((mask, one)):
                    rhs[plane, at:at + size, :wide] = x * factor
                    rhs[plane, at:at + size, wide:] = jnp.where(lane[:size] < 3, factor, 0.0)
                at += gap
    factors = [rhs[plane].astype(BF16) for plane in range(2)]

    lane = lax.broadcasted_iota(jnp.int32, (chans, cols), 1)
    pair_out = out_ref[...]
    high = pbias_ref[...].astype(BF16).astype(F32)
    rest = pbias_ref[...] - high
    middle = rest.astype(BF16).astype(F32)
    bias_parts = jnp.where(
        lane == 0, high, jnp.where(lane == 1, middle, jnp.where(lane == 2, rest - middle, 0.0))
    ).astype(BF16)
    last_two, first_two = lane >= cols - REACH, lane < REACH

    def features(rounded, places, plane):
        scaled = jnp.concatenate([pair_out * rounded[j:j + 1] for j in range(len(places))], axis=0)
        scaled = jnp.concatenate(
            [scaled.astype(BF16), jnp.concatenate([bias_parts] * len(places), axis=0)], axis=1
        )
        values = lax.dot_general(scaled, factors[plane], ROWS_BY_COLS, preferred_element_type=F32)
        for j, place in enumerate(places):
            for side, i in enumerate(place):
                value = values[j * chans:(j + 1) * chans, side * width:(side + 1) * width]
                own, beside = value[:, :cols], value[:, cols:]
                if plane == 0:
                    feat[i // 2, :, (i % 2) * cols:(i % 2 + 1) * cols] = own
                else:
                    zone = 6 if i < 0 else 8
                    own = own * misc_ref[zone:zone + 1, :]
                    beside = beside * misc_ref[zone + 1:zone + 2, :]
                own, beside = (jnp.maximum(x.astype(BF16), 0) for x in (own, beside))
                before = pltpu.roll(jnp.where(last_two, beside, own), REACH, 1)
                after = pltpu.roll(jnp.where(first_two, beside, own), cols - REACH, 1)
                at = slice((i + REACH) * cols, (i + REACH + 1) * cols)
                hid[0:chans, at] = before.astype(BF16)
                hid[chans:2 * chans, at] = own.astype(BF16)
                hid[2 * chans:3 * chans, at] = after.astype(BF16)

    def rounded(x):
        return x.astype(BF16).astype(F32)

    features(rounded(misc_ref[REACH:2 * REACH, :]), [(rows + j, j - REACH) for j in range(REACH)], 1)
    for m in range(0, half, GROUP):
        features(rounded(row_ref[m:m + GROUP, :]), [(m + j, half + m + j) for j in range(GROUP)], 0)
        if (2 * m) % 16 == 0:
            turned_target[2 * m:2 * m + 16] = jnp.swapaxes(target_ref[:, 2 * m:2 * m + 16, :], 0, 1)

    zero = jnp.zeros((chans, width), BF16)
    for tap, e in ((0, pairs - 2), (0, pairs - 1), (1, 0), (1, pairs - 1), (2, 0), (2, 1)):
        dif_taps[tap * chans:(tap + 1) * chans, e * width:(e + 1) * width] = zero
    cbias = jnp.broadcast_to(cbias_ref[...], (chans, width))
    keep = jnp.concatenate([misc_ref[4:5, :]] * 2, axis=1)
    bias_sum = jnp.zeros((chans, width), F32)
    for e in range(pairs):
        part = jnp.dot(weight_ref[...], hid[:, e * width:(e + 1) * width], preferred_element_type=F32)
        m = e - 2
        if m >= 0:
            target = jnp.concatenate([turned_target[2 * m], turned_target[2 * m + 1]], axis=1).astype(F32)
            out = near + part[2 * chans:]
            differ = keep * (feat[m] + (out + cbias) - target)
            loss = 0.5 * jnp.sum(differ * differ, axis=0, keepdims=True)
            loss_ref[2 * m:2 * m + 1, :] = loss[:, :cols]
            loss_ref[2 * m + 1:2 * m + 2, :] = loss[:, cols:]
            bias_sum = bias_sum + differ
            grad_in = differ.astype(BF16)
            for tap in range(3):
                dif_taps[tap * chans:(tap + 1) * chans, (m + tap) * width:(m + tap + 1) * width] = grad_in
        if e > 0:
            near = far + part[chans:2 * chans]
        far = part[0:chans]

    grad = lax.dot_general(hid[...], dif_taps[...], ROWS_BY_COLS, preferred_element_type=F32) * norm
    split = taps // 2
    grad_ref[0:taps, :] = grad[:, 0:2 * chans]
    last = grad[:, 2 * chans:]
    grad_ref[taps:taps + split, :] = jnp.concatenate([last[:split], last[split:]], axis=1)
    sums = bias_sum[:, :cols] + bias_sum[:, cols:]
    bias = lax.dot_general(
        jnp.ones((8, cols), F32), sums, ROWS_BY_COLS, preferred_element_type=F32, precision=lax.Precision.HIGHEST
    )
    grad_ref[taps + split:, :] = jnp.zeros((grad_ref.shape[0] - taps - split, 2 * chans), F32)
    grad_ref[taps + split:taps + split + 8, 0:chans] = bias * norm


def unpack_kernel(own_ref, other_ref, conv_ref, bias_ref):
    chans = conv_ref.shape[3]
    first = lax.axis_index("rep") == 0
    own, other = own_ref[...], other_ref[...]
    whole = jnp.concatenate([jnp.where(first, own, other), jnp.where(first, other, own)], axis=0)
    taps, split = 3 * chans, 3 * chans // 2
    for a in range(2):
        for b in range(3):
            conv_ref[a, b] = whole[b * chans:(b + 1) * chans, a * chans:(a + 1) * chans]
    last = jnp.concatenate([whole[taps:taps + split, :chans], whole[taps:taps + split, chans:]], axis=0)
    for b in range(3):
        conv_ref[2, b] = last[b * chans:(b + 1) * chans]
    bias_ref[...] = whole[taps + split:taps + split + 1, :chans]


GROUP = 8


def per_device(
    emb_row, emb_col, proj_row, proj_col, pair_out, pair_bias, conv_weight, conv_bias, target, kept_tiles
):
    chans, rows, cols = target.shape
    rank = pair_out.shape[0]
    row, col, rep = (lax.axis_index(axis) for axis in MESH)
    n_row, n_col, n_rep = (lax.axis_size(axis) for axis in MESH)
    edge = rows // kept_tiles.shape[0]
    half, wide = rows // 2, 2 * rank
    vmem = pl.BlockSpec(memory_space=pltpu.VMEM)

    shares = emb_row.shape[1], emb_col.shape[1]
    sliced = (shares[0] % 128 == 0, shares[1] % 16 == 0)
    projs = [proj_row.T, proj_col.T]
    for side, place in enumerate((col, row)):
        if not sliced[side]:
            projs[side] = lax.dynamic_slice_in_dim(projs[side], place * shares[side], shares[side], 1)
    zeros = pl.pallas_call(
        zeros_kernel,
        out_shape=jax.ShapeDtypeStruct((8, wide), F32),
        out_specs=vmem,
        compiler_params=pltpu.CompilerParams(vmem_limit_bytes=4 * 1024 * 1024),
        cost_estimate=pl.CostEstimate(flops=4 * 10**9, bytes_accessed=1000, transcendentals=0),
        name="zeros",
    )()
    col_send, row_send, ends_send = pl.pallas_call(
        functools.partial(project_kernel, sliced=sliced),
        out_shape=(
            jax.ShapeDtypeStruct((half + 8, wide), F32),
            jax.ShapeDtypeStruct((half + 8, wide), F32),
            jax.ShapeDtypeStruct((8, wide), F32),
        ),
        in_specs=[vmem] * 6,
        out_specs=(vmem,) * 3,
        scratch_shapes=[pltpu.VMEM((projs[1].shape[1], cols), BF16)],
        compiler_params=pltpu.CompilerParams(vmem_limit_bytes=4 * 1024 * 1024),
        cost_estimate=pl.CostEstimate(flops=2 * 10**9, bytes_accessed=1000, transcendentals=0),
        name="project",
    )(zeros, kept_tiles, emb_row, projs[0], emb_col.T, projs[1])

    def shifted(x, k, row, rep):
        return send(x, lambda r, c, p: (r ^ row, (c + k) % n_col, p ^ rep))

    from_cross = {k: shifted(ends_send, k, 1, 0) for k in range(1, n_col)}
    from_mates = {k: shifted(ends_send, k, 0, 1) for k in range(1, n_col)}
    from_row = swap(row_send, row=1)

    lane = lax.broadcasted_iota(jnp.int32, (1, wide), 1)
    lower = lane < rank

    def sides(blocks, at, size):
        return jnp.where(lower, blocks[n_col - 1][at:at + size], blocks[1][at:at + size])

    def masks(kept, blocks, at):
        beside = jnp.where(jnp.where(lower, col < n_col - 1, col > 0), sides(blocks, at, 1), 0.0)
        return jnp.concatenate([kept, beside], axis=0)

    col_sum = row_send[:half] + from_row[:half]
    side = sides(from_mates, REACH + 1, REACH) + sides(from_cross, REACH + 1, REACH)
    block = jnp.concatenate(
        [
            from_row[half:half + REACH] + sum(from_cross[k][:REACH] for k in from_cross),
            masks(from_row[half + REACH:half + REACH + 1], from_cross, REACH),
        ],
        axis=0,
    )

    from_col = {k: shifted(col_send, k, 0, 0) for k in range(1, n_col)}
    row_sum = col_send[:half] + sum(from_col[k][:half] for k in from_col)
    own_masks = masks(col_send[half:half + 1], from_col, half)

    mate = swap(jnp.concatenate([ends_send[:REACH + 2], block], axis=0), rep=1)
    mate_ends = mate[:REACH] + sum(from_mates[k][:REACH] for k in from_mates)
    mate_masks = masks(mate[REACH:REACH + 1], from_mates, REACH)

    blocks = {1: mate[REACH + 2:]}
    pad = jnp.zeros((2, wide), F32)
    for step in steps("row", 2):
        got = swap(jnp.concatenate([col_sum, side, block, pad], axis=0), row=step, rep=1 if step == 2 else 0)
        col_sum = col_sum + got[:half]
        side = side + got[half:half + REACH]
        block = got[half + REACH:half + REACH + 4]
        blocks[2 * step - 1] = block

    beyond = jnp.where(rep == 0, row - 1, row + 1)
    far = blocks[1]
    for apart, found in blocks.items():
        far = jnp.where((row ^ beyond) == apart, found, far)
    far_masks = jnp.where((beyond >= 0) & (beyond < n_row), far[REACH:], 0.0)
    above = jnp.where(rep == 0, far[:REACH], mate_ends)
    below = jnp.where(rep == 0, mate_ends, far[:REACH])
    misc = jnp.concatenate(
        [
            side,
            jnp.where(lower, below, above),
            own_masks,
            jnp.where(rep == 0, far_masks, mate_masks),
            jnp.where(rep == 0, mate_masks, far_masks),
            jnp.zeros((6, wide), F32),
        ],
        axis=0,
    )

    cells = (rows + 2 * REACH) * cols
    taps = 3 * chans
    weight = conv_weight.transpose(0, 3, 1, 2).reshape(taps, taps)
    packed = taps + taps // 2 + 16
    out_t = pair_out.astype(F32).T
    cell_loss, grads = pl.pallas_call(
        functools.partial(tile_kernel, norm=1.0 / (edge * edge)),
        out_shape=(
            jax.ShapeDtypeStruct((rows, cols), F32),
            jax.ShapeDtypeStruct((packed, 2 * chans), F32),
        ),
        in_specs=[vmem] * 8,
        out_specs=(vmem,) * 2,
        scratch_shapes=[
            pltpu.VMEM((taps, cells), BF16),
            pltpu.VMEM((taps, cells), BF16),
            pltpu.VMEM((rows // 2, chans, 2 * cols), F32),
            pltpu.VMEM((2, 4 * cols, 2 * wide), F32),
            pltpu.VMEM((rows, chans, cols), BF16),
        ],
        compiler_params=pltpu.CompilerParams(vmem_limit_bytes=40 * 1024 * 1024),
        name="tile",
    )(
        row_sum, col_sum, misc, jnp.concatenate([out_t, out_t], axis=1), pair_bias[:, None], weight,
        conv_bias[:, None], target,
    )

    piece = packed // n_rep
    mine = lax.dynamic_slice_in_dim(grads, rep * piece, piece, 0)
    total = mine + swap(lax.dynamic_slice_in_dim(grads, (1 - rep) * piece, piece, 0), rep=1)
    corner = swap(total, row=1, col=1)
    beside = swap(total, col=1)
    total = (total + beside) + (swap(total, row=1) + corner)
    for step in steps("col", 2):
        total = total + swap(total, col=step)
    for step in steps("row", 2):
        total = total + swap(total, row=step)
    other = swap(total, rep=1)
    grad_conv, grad_bias = pl.pallas_call(
        unpack_kernel,
        out_shape=(jax.ShapeDtypeStruct((3, 3, chans, chans), F32), jax.ShapeDtypeStruct((1, chans), F32)),
        in_specs=[vmem] * 2,
        out_specs=(vmem,) * 2,
        compiler_params=pltpu.CompilerParams(vmem_limit_bytes=4 * 1024 * 1024),
        name="unpack",
    )(total, other)
    return cell_loss, grad_conv, grad_bias[0]


def solution(mesh):
    in_specs = (
        P(("grp", "row", "rep"), "col"),
        P(("grp", "col"), "row"),
        P(),
        P(),
        P(),
        P(),
        P(),
        P(),
        P(None, ("grp", "row", "rep"), "col"),
        P(("grp", "row", "rep"), "col"),
    )
    out_specs = (P(("grp", "row", "rep"), "col"), P("grp", None, None, None), P("grp"))
    return jax.shard_map(
        per_device, mesh=mesh, in_specs=in_specs, out_specs=out_specs, check_vma=False
    )
```

```python
import functools

import jax
import jax.numpy as jnp
from jax import lax
from jax.experimental import pallas as pl
from jax.experimental.pallas import tpu as pltpu
from jax.sharding import PartitionSpec as P

REACH = 2
F32 = jnp.float32
BF16 = jnp.bfloat16
ROWS_BY_COLS = (((1,), (1,)), ((), ()))
MESH = ("row", "col", "rep")


def send(x, target):
    sizes = [lax.axis_size(axis) for axis in MESH]

    def index(r, c, p):
        return (r * sizes[1] + c) * sizes[2] + p

    places = [(r, c, p) for r in range(sizes[0]) for c in range(sizes[1]) for p in range(sizes[2])]
    return lax.ppermute(x, MESH, [(index(*place), index(*target(*place))) for place in places])


def swap(x, row=0, col=0, rep=0):
    return send(x, lambda r, c, p: (r ^ row, c ^ col, p ^ rep))


def steps(axis, first=1):
    step = first
    while step < lax.axis_size(axis):
        yield step
        step *= 2


def zeros_kernel(zeros_ref):
    zeros_ref[...] = jnp.zeros_like(zeros_ref)


def project_kernel(
    zeros_ref, kept_ref, row_ref, row_proj_ref, col_ref, col_proj_ref,
    col_send_ref, row_send_ref, ends_send_ref, col_wide, *, sliced
):
    row_at = col_at = 0
    depth = row_ref.shape[1]
    if sliced[0]:
        row_at = pl.multiple_of(lax.axis_index("col") * depth, 128)
    if sliced[1]:
        col_at = pl.multiple_of(lax.axis_index("row") * col_ref.shape[0], 16)
    col_wide[...] = jnp.zeros_like(col_wide)
    col_wide[pl.ds(col_at, col_ref.shape[0]), :] = col_ref[...]
    half, wide = row_ref.shape[0] // 2, 2 * row_proj_ref.shape[0]
    lane = lax.broadcasted_iota(jnp.int32, (REACH, wide), 1)

    def packed(x):
        return jnp.concatenate([x[:half], x[half:]], axis=1)

    def ends(x):
        return jnp.where(lane < wide // 2, x[:REACH], x[half - REACH:])

    kept = jnp.broadcast_to(kept_ref[...].astype(F32), (1, wide))
    rows = packed(
        lax.dot_general(
            row_ref[...], row_proj_ref[:, pl.ds(row_at, depth)], ROWS_BY_COLS, preferred_element_type=F32
        )
    )
    cols = packed(jnp.dot(col_proj_ref[...], col_wide[...], preferred_element_type=F32).T)
    row_ends, col_ends = ends(rows), ends(cols)
    zero = zeros_ref[...]
    col_send_ref[0:half, :] = rows
    row_send_ref[0:half, :] = cols
    col_send_ref[half:, :] = jnp.concatenate([kept, zero[:7]], axis=0)
    row_send_ref[half:, :] = jnp.concatenate([row_ends, kept, zero[:5]], axis=0)
    ends_send_ref[...] = jnp.concatenate([row_ends, kept, col_ends, zero[:3]], axis=0)


def tile_kernel(
    row_ref, col_ref, misc_ref, out_ref, pbias_ref, weight_ref, cbias_ref, target_ref,
    loss_ref, grad_ref, hid, dif_taps, feat, rhs, turned_target, *, norm
):
    chans, rows, cols = target_ref.shape
    half, wide = row_ref.shape
    rank = wide // 2
    width = 2 * cols
    pairs = rows // 2 + 2
    taps = weight_ref.shape[0]

    kept = misc_ref[4:5, 0:1]
    lane = lax.broadcasted_iota(jnp.int32, (half, wide), 1)
    rhs[...] = jnp.zeros_like(rhs)
    after_map, before_map = misc_ref[5:6, 0:1], misc_ref[5:6, wide - 1:wide]
    one = jnp.ones((1, 1), F32)
    pieces = ((0, col_ref[...], half, kept, kept), (cols, misc_ref[0:REACH, :], cols - REACH, after_map, before_map))
    for start, value, gap, mask_first, mask_last in pieces:
        turned = pltpu.roll(value, rank, 1)
        size = value.shape[0]
        lower = lane[:size] < rank
        for base, first, last in ((0, value, turned), (2 * cols, turned, value)):
            keep_half = lower if base == 0 else ~lower
            at = base + start
            for x, mask in ((first, mask_first), (last, mask_last)):
                x = jnp.where(keep_half, x, 0.0)
                for plane, factor in enumerate((mask, one)):
                    rhs[plane, at:at + size, :wide] = x * factor
                    rhs[plane, at:at + size, wide:] = jnp.where(lane[:size] < 3, factor, 0.0)
                at += gap
    factors = [rhs[plane].astype(BF16) for plane in range(2)]

    lane = lax.broadcasted_iota(jnp.int32, (chans, cols), 1)
    pair_out = out_ref[...]
    high = pbias_ref[...].astype(BF16).astype(F32)
    rest = pbias_ref[...] - high
    middle = rest.astype(BF16).astype(F32)
    bias_parts = jnp.where(
        lane == 0, high, jnp.where(lane == 1, middle, jnp.where(lane == 2, rest - middle, 0.0))
    ).astype(BF16)
    last_two, first_two = lane >= cols - REACH, lane < REACH

    def features(rounded, places, plane):
        scaled = jnp.concatenate([pair_out * rounded[j:j + 1] for j in range(len(places))], axis=0)
        scaled = jnp.concatenate(
            [scaled.astype(BF16), jnp.concatenate([bias_parts] * len(places), axis=0)], axis=1
        )
        values = lax.dot_general(scaled, factors[plane], ROWS_BY_COLS, preferred_element_type=F32)
        for j, place in enumerate(places):
            for side, i in enumerate(place):
                value = values[j * chans:(j + 1) * chans, side * width:(side + 1) * width]
                own, beside = value[:, :cols], value[:, cols:]
                if plane == 0:
                    feat[i // 2, :, (i % 2) * cols:(i % 2 + 1) * cols] = own
                else:
                    zone = 6 if i < 0 else 8
                    own = own * misc_ref[zone:zone + 1, :]
                    beside = beside * misc_ref[zone + 1:zone + 2, :]
                own, beside = (jnp.maximum(x.astype(BF16), 0) for x in (own, beside))
                before = pltpu.roll(jnp.where(last_two, beside, own), REACH, 1)
                after = pltpu.roll(jnp.where(first_two, beside, own), cols - REACH, 1)
                at = slice((i + REACH) * cols, (i + REACH + 1) * cols)
                hid[0:chans, at] = before.astype(BF16)
                hid[chans:2 * chans, at] = own.astype(BF16)
                hid[2 * chans:3 * chans, at] = after.astype(BF16)

    def rounded(x):
        return x.astype(BF16).astype(F32)

    features(rounded(misc_ref[REACH:2 * REACH, :]), [(rows + j, j - REACH) for j in range(REACH)], 1)
    for m in range(0, half, GROUP):
        features(rounded(row_ref[m:m + GROUP, :]), [(m + j, half + m + j) for j in range(GROUP)], 0)
        if (2 * m) % 16 == 0:
            turned_target[2 * m:2 * m + 16] = jnp.swapaxes(target_ref[:, 2 * m:2 * m + 16, :], 0, 1)

    zero = jnp.zeros((chans, width), BF16)
    for tap, e in ((0, pairs - 2), (0, pairs - 1), (1, 0), (1, pairs - 1), (2, 0), (2, 1)):
        dif_taps[tap * chans:(tap + 1) * chans, e * width:(e + 1) * width] = zero
    cbias = jnp.broadcast_to(cbias_ref[...], (chans, width))
    keep = jnp.concatenate([misc_ref[4:5, :]] * 2, axis=1)
    bias_sum = jnp.zeros((chans, width), F32)
    joined = 3 if pairs % 3 == 0 else 1
    for e in range(pairs):
        if e % joined == 0:
            parts = jnp.dot(weight_ref[...], hid[:, e * width:(e + joined) * width], preferred_element_type=F32)
        part = parts[:, e % joined * width:(e % joined + 1) * width]
        m = e - 2
        if m >= 0:
            target = jnp.concatenate([turned_target[2 * m], turned_target[2 * m + 1]], axis=1).astype(F32)
            out = near + part[2 * chans:]
            differ = keep * (feat[m] + (out + cbias) - target)
            loss = 0.5 * jnp.sum(differ * differ, axis=0, keepdims=True)
            loss_ref[2 * m:2 * m + 1, :] = loss[:, :cols]
            loss_ref[2 * m + 1:2 * m + 2, :] = loss[:, cols:]
            bias_sum = bias_sum + differ
            grad_in = differ.astype(BF16)
            for tap in range(3):
                dif_taps[tap * chans:(tap + 1) * chans, (m + tap) * width:(m + tap + 1) * width] = grad_in
        if e > 0:
            near = far + part[chans:2 * chans]
        far = part[0:chans]

    grad = lax.dot_general(hid[...], dif_taps[...], ROWS_BY_COLS, preferred_element_type=F32) * norm
    split = taps // 2
    grad_ref[0:taps, :] = grad[:, 0:2 * chans]
    last = grad[:, 2 * chans:]
    grad_ref[taps:taps + split, :] = jnp.concatenate([last[:split], last[split:]], axis=1)
    sums = bias_sum[:, :cols] + bias_sum[:, cols:]
    bias = lax.dot_general(
        jnp.ones((8, cols), F32), sums, ROWS_BY_COLS, preferred_element_type=F32, precision=lax.Precision.HIGHEST
    )
    grad_ref[taps + split:, :] = jnp.zeros((grad_ref.shape[0] - taps - split, 2 * chans), F32)
    grad_ref[taps + split:taps + split + 8, 0:chans] = bias * norm


def unpack_kernel(own_ref, other_ref, conv_ref, bias_ref):
    chans = conv_ref.shape[3]
    first = lax.axis_index("rep") == 0
    own, other = own_ref[...], other_ref[...]
    whole = jnp.concatenate([jnp.where(first, own, other), jnp.where(first, other, own)], axis=0)
    taps, split = 3 * chans, 3 * chans // 2
    for a in range(2):
        for b in range(3):
            conv_ref[a, b] = whole[b * chans:(b + 1) * chans, a * chans:(a + 1) * chans]
    last = jnp.concatenate([whole[taps:taps + split, :chans], whole[taps:taps + split, chans:]], axis=0)
    for b in range(3):
        conv_ref[2, b] = last[b * chans:(b + 1) * chans]
    bias_ref[...] = whole[taps + split:taps + split + 1, :chans]


GROUP = 4


def per_device(
    emb_row, emb_col, proj_row, proj_col, pair_out, pair_bias, conv_weight, conv_bias, target, kept_tiles
):
    chans, rows, cols = target.shape
    rank = pair_out.shape[0]
    row, col, rep = (lax.axis_index(axis) for axis in MESH)
    n_row, n_col, n_rep = (lax.axis_size(axis) for axis in MESH)
    edge = rows // kept_tiles.shape[0]
    half, wide = rows // 2, 2 * rank
    vmem = pl.BlockSpec(memory_space=pltpu.VMEM)

    shares = emb_row.shape[1], emb_col.shape[1]
    sliced = (shares[0] % 128 == 0, shares[1] % 16 == 0)
    projs = [proj_row.T, proj_col.T]
    for side, place in enumerate((col, row)):
        if not sliced[side]:
            projs[side] = lax.dynamic_slice_in_dim(projs[side], place * shares[side], shares[side], 1)
    zeros = pl.pallas_call(
        zeros_kernel,
        out_shape=jax.ShapeDtypeStruct((8, wide), F32),
        out_specs=vmem,
        compiler_params=pltpu.CompilerParams(vmem_limit_bytes=4 * 1024 * 1024),
        cost_estimate=pl.CostEstimate(flops=4 * 10**9, bytes_accessed=1000, transcendentals=0),
        name="zeros",
    )()
    col_send, row_send, ends_send = pl.pallas_call(
        functools.partial(project_kernel, sliced=sliced),
        out_shape=(
            jax.ShapeDtypeStruct((half + 8, wide), F32),
            jax.ShapeDtypeStruct((half + 8, wide), F32),
            jax.ShapeDtypeStruct((8, wide), F32),
        ),
        in_specs=[vmem] * 6,
        out_specs=(vmem,) * 3,
        scratch_shapes=[pltpu.VMEM((projs[1].shape[1], cols), BF16)],
        compiler_params=pltpu.CompilerParams(vmem_limit_bytes=4 * 1024 * 1024),
        cost_estimate=pl.CostEstimate(flops=2 * 10**9, bytes_accessed=1000, transcendentals=0),
        name="project",
    )(zeros, kept_tiles, emb_row, projs[0], emb_col.T, projs[1])

    def shifted(x, k, row, rep):
        return send(x, lambda r, c, p: (r ^ row, (c + k) % n_col, p ^ rep))

    from_cross = {k: shifted(ends_send, k, 1, 0) for k in range(1, n_col)}
    from_mates = {k: shifted(ends_send, k, 0, 1) for k in range(1, n_col)}
    from_row = swap(row_send, row=1)

    lane = lax.broadcasted_iota(jnp.int32, (1, wide), 1)
    lower = lane < rank

    def sides(blocks, at, size):
        return jnp.where(lower, blocks[n_col - 1][at:at + size], blocks[1][at:at + size])

    def masks(kept, blocks, at):
        beside = jnp.where(jnp.where(lower, col < n_col - 1, col > 0), sides(blocks, at, 1), 0.0)
        return jnp.concatenate([kept, beside], axis=0)

    col_sum = row_send[:half] + from_row[:half]
    side = sides(from_mates, REACH + 1, REACH) + sides(from_cross, REACH + 1, REACH)
    block = jnp.concatenate(
        [
            from_row[half:half + REACH] + sum(from_cross[k][:REACH] for k in from_cross),
            masks(from_row[half + REACH:half + REACH + 1], from_cross, REACH),
        ],
        axis=0,
    )

    from_col = {k: shifted(col_send, k, 0, 0) for k in range(1, n_col)}
    row_sum = col_send[:half] + sum(from_col[k][:half] for k in from_col)
    own_masks = masks(col_send[half:half + 1], from_col, half)

    mate = swap(jnp.concatenate([ends_send[:REACH + 2], block], axis=0), rep=1)
    mate_ends = mate[:REACH] + sum(from_mates[k][:REACH] for k in from_mates)
    mate_masks = masks(mate[REACH:REACH + 1], from_mates, REACH)

    blocks = {1: mate[REACH + 2:]}
    pad = jnp.zeros((2, wide), F32)
    for step in steps("row", 2):
        got = swap(jnp.concatenate([col_sum, side, block, pad], axis=0), row=step, rep=1 if step == 2 else 0)
        col_sum = col_sum + got[:half]
        side = side + got[half:half + REACH]
        block = got[half + REACH:half + REACH + 4]
        blocks[2 * step - 1] = block

    beyond = jnp.where(rep == 0, row - 1, row + 1)
    far = blocks[1]
    for apart, found in blocks.items():
        far = jnp.where((row ^ beyond) == apart, found, far)
    far_masks = jnp.where((beyond >= 0) & (beyond < n_row), far[REACH:], 0.0)
    above = jnp.where(rep == 0, far[:REACH], mate_ends)
    below = jnp.where(rep == 0, mate_ends, far[:REACH])
    misc = jnp.concatenate(
        [
            side,
            jnp.where(lower, below, above),
            own_masks,
            jnp.where(rep == 0, far_masks, mate_masks),
            jnp.where(rep == 0, mate_masks, far_masks),
            jnp.zeros((6, wide), F32),
        ],
        axis=0,
    )

    cells = (rows + 2 * REACH) * cols
    taps = 3 * chans
    weight = conv_weight.transpose(0, 3, 1, 2).reshape(taps, taps)
    packed = taps + taps // 2 + 16
    out_t = pair_out.astype(F32).T
    cell_loss, grads = pl.pallas_call(
        functools.partial(tile_kernel, norm=1.0 / (edge * edge)),
        out_shape=(
            jax.ShapeDtypeStruct((rows, cols), F32),
            jax.ShapeDtypeStruct((packed, 2 * chans), F32),
        ),
        in_specs=[vmem] * 8,
        out_specs=(vmem,) * 2,
        scratch_shapes=[
            pltpu.VMEM((taps, cells), BF16),
            pltpu.VMEM((taps, cells), BF16),
            pltpu.VMEM((rows // 2, chans, 2 * cols), F32),
            pltpu.VMEM((2, 4 * cols, 2 * wide), F32),
            pltpu.VMEM((rows, chans, cols), BF16),
        ],
        compiler_params=pltpu.CompilerParams(vmem_limit_bytes=40 * 1024 * 1024),
        name="tile",
    )(
        row_sum, col_sum, misc, jnp.concatenate([out_t, out_t], axis=1), pair_bias[:, None], weight,
        conv_bias[:, None], target,
    )

    piece = packed // n_rep
    mine = lax.dynamic_slice_in_dim(grads, rep * piece, piece, 0)
    total = mine + swap(lax.dynamic_slice_in_dim(grads, (1 - rep) * piece, piece, 0), rep=1)
    corner = swap(total, row=1, col=1)
    beside = swap(total, col=1)
    total = (total + beside) + (swap(total, row=1) + corner)
    for step in steps("col", 2):
        total = total + swap(total, col=step)
    for step in steps("row", 2):
        total = total + swap(total, row=step)
    other = swap(total, rep=1)
    grad_conv, grad_bias = pl.pallas_call(
        unpack_kernel,
        out_shape=(jax.ShapeDtypeStruct((3, 3, chans, chans), F32), jax.ShapeDtypeStruct((1, chans), F32)),
        in_specs=[vmem] * 2,
        out_specs=(vmem,) * 2,
        compiler_params=pltpu.CompilerParams(vmem_limit_bytes=4 * 1024 * 1024),
        name="unpack",
    )(total, other)
    return cell_loss, grad_conv, grad_bias[0]


def solution(mesh):
    in_specs = (
        P(("grp", "row", "rep"), "col"),
        P(("grp", "col"), "row"),
        P(),
        P(),
        P(),
        P(),
        P(),
        P(),
        P(None, ("grp", "row", "rep"), "col"),
        P(("grp", "row", "rep"), "col"),
    )
    out_specs = (P(("grp", "row", "rep"), "col"), P("grp", None, None, None), P("grp"))
    return jax.shard_map(
        per_device, mesh=mesh, in_specs=in_specs, out_specs=out_specs, check_vma=False
    )
```
